768 devices in a mesh: region: 12 (over z), local: 64 (over x, y, core).
Axes of the slice: x: 4, y: 8, z: 12, core: 2. Of those that a mesh axis runs over, the one named last changes fastest.
Arguments:
- populations: float32 [19, 256, 192, 256], P(None, 'local', 'region'), may hold values from 0.005 to 0.5, as said below
- fluid_mask: int32 [256, 192, 256], P('local', 'region'), may hold values from 0 to 1, as said below
Outputs:
- advanced: float32 [19, 256, 192, 256], P(None, 'local', 'region')
The draws below stay inside these ranges and needn't reach their ends.
Inputs may be any that keep to these rules, and one draw needn't show every extreme that they name: `fluid_mask`: 1 marks fluid and 0 wall; the fluid sites form one vessel along the second dimension whose rough wall runs close to the grid's sides in the first and third dimensions. `populations`: positive distributions near a local equilibrium.
All inputs are finite; a program needn't handle non-finite values.
Results may differ from the reference program's by a relative error of at most 0.0003.
Values sent between devices are 32-bit elements; how exact they have to be, the bound alone decides.
No kernel may reach another device: no remote copies, remote signals or barrier semaphores. Data moves between devices by JAX's collectives and lax.ppermute only.
A program may use at most 32 MiB of HBM per device.

```python
import jax
import jax.numpy as jnp

NZ = 256
STEPS = 2
NX = 256
NY = 192


VELOCITIES = ((0, 0, 0), (1, 0, 0), (-1, 0, 0), (0, 1, 0), (0, -1, 0), (0, 0, 1), (0, 0, -1), (1, 1, 0), (-1, -1, 0), (1, -1, 0), (-1, 1, 0), (1, 0, 1), (-1, 0, -1), (1, 0, -1), (-1, 0, 1), (0, 1, 1), (0, -1, -1), (0, 1, -1), (0, -1, 1))


WEIGHTS = (1.0 / 3.0,) + (1.0 / 18.0,) * 6 + (1.0 / 36.0,) * 12


def draw_populations(key, part):
    key = jax.random.fold_in(key, 11)
    speed_key, noise_key, mass_key = jax.random.split(key, 3)
    across_x = (2.0 * jnp.arange(NX, dtype=jnp.float32) - (NX - 1)) / NX
    across_z = (2.0 * jnp.arange(NZ, dtype=jnp.float32) - (NZ - 1)) / NZ
    radial = across_x[:, None, None] * across_x[:, None, None] + across_z[None, None, :] * across_z[None, None, :]
    profile = jnp.maximum(1.0 - radial * radial, 0.0)
    lateral = (jnp.arange(NX, dtype=jnp.float32) + 0.5) / NX
    lengthwise = (jnp.arange(NY, dtype=jnp.float32) + 0.5) / NY
    speed = jax.random.uniform(speed_key, (), jnp.float32, 0.03, 0.07)
    tilt = 0.4 + 1.2 * lateral
    along = 0.5 + lengthwise
    noise = jnp.clip(0.1 * jax.random.normal(noise_key, (19, NX, NY, NZ), jnp.float32), -0.3, 0.3)
    mass = 1.0 + jnp.clip(0.03 * jax.random.normal(mass_key, (NX, NY, NZ), jnp.float32), -0.09, 0.09)
    flow = speed * tilt[:, None, None] * along[None, :, None] * profile
    square = flow * flow
    result = []
    for number in range(19):
        projected = VELOCITIES[number][1] * flow
        equil = WEIGHTS[number] * mass * (1.0 + 3.0 * projected + 4.5 * projected * projected - 1.5 * square)
        result.append(equil * (1.0 + noise[number]))
    return jnp.stack(result)


def draw_fluid_mask(key, part):
    key = jax.random.fold_in(key, 5)
    grid_x = (2 * jnp.arange(NX, dtype=jnp.int32) - (NX - 1)) * 256 // NX
    grid_z = (2 * jnp.arange(NZ, dtype=jnp.int32) - (NZ - 1)) * 256 // NZ
    radial = grid_x[:, None, None] * grid_x[:, None, None] + grid_z[None, None, :] * grid_z[None, None, :]
    rough = jax.random.randint(key, (NX, NY, NZ), 0, 6000, dtype=jnp.int32)
    return (radial + rough <= 65536).astype(jnp.int32)


def setup_inputs(seed: int = 0) -> dict:
    streams_of = jax.random.split(jax.random.key(seed), 3)
    return {
        "populations": draw_populations(jax.random.fold_in(streams_of[2], 71), 0),
        "fluid_mask": draw_fluid_mask(jax.random.fold_in(streams_of[2], 71), 0),
    }


VELOCITIES = ((0, 0, 0), (1, 0, 0), (-1, 0, 0), (0, 1, 0), (0, -1, 0), (0, 0, 1), (0, 0, -1),
              (1, 1, 0), (-1, -1, 0), (1, -1, 0), (-1, 1, 0), (1, 0, 1), (-1, 0, -1), (1, 0, -1),
              (-1, 0, 1), (0, 1, 1), (0, -1, -1), (0, 1, -1), (0, -1, 1))
WEIGHTS = (1.0 / 3.0,) + (1.0 / 18.0,) * 6 + (1.0 / 36.0,) * 12
RELAX = 0.8
GAIN_RATE = 2.0
TARGET_SPEED = 0.05


def opposite_of(number):
    if number == 0:
        return 0
    return number + 1 if number % 2 == 1 else number - 1


def moments(current):
    density = jnp.sum(current, axis=0)
    flux_x = current[1] - current[2]
    flux_y = current[3] - current[4]
    flux_z = current[5] - current[6]
    for number in range(7, 19):
        move_x, move_y, move_z = VELOCITIES[number]
        if move_x != 0:
            flux_x = flux_x + move_x * current[number]
        if move_y != 0:
            flux_y = flux_y + move_y * current[number]
        if move_z != 0:
            flux_z = flux_z + move_z * current[number]
    return density, flux_x, flux_y, flux_z


def collide(current, fluid, forcing):
    density, flux_x, flux_y, flux_z = moments(current)
    safe = density + (1.0 - fluid)
    speed_x = flux_x / safe
    speed_y = flux_y / safe + RELAX * forcing
    speed_z = flux_z / safe
    square = speed_x * speed_x + speed_y * speed_y + speed_z * speed_z
    result = []
    for number in range(19):
        move_x, move_y, move_z = VELOCITIES[number]
        projected = move_x * speed_x + move_y * speed_y + move_z * speed_z
        equil = WEIGHTS[number] * density * (1.0 + 3.0 * projected + 4.5 * projected * projected - 1.5 * square)
        result.append(fluid * (current[number] - (current[number] - equil) / RELAX))
    return jnp.stack(result)


def stream(post, fluid):
    size_x = post.shape[1] - 2
    size_y = post.shape[2] - 2
    size_z = post.shape[3]
    padded = jnp.pad(post, ((0, 0), (0, 0), (0, 0), (1, 1)))
    padded_fluid = jnp.pad(fluid, ((0, 0), (0, 0), (1, 1)))
    center = padded_fluid[1:1 + size_x, 1:1 + size_y, 1:1 + size_z]
    result = []
    for number in range(19):
        move_x, move_y, move_z = VELOCITIES[number]
        source = padded[number, 1 - move_x:1 - move_x + size_x, 1 - move_y:1 - move_y + size_y,
                        1 - move_z:1 - move_z + size_z]
        source_fluid = padded_fluid[1 - move_x:1 - move_x + size_x, 1 - move_y:1 - move_y + size_y,
                                    1 - move_z:1 - move_z + size_z]
        own = post[opposite_of(number), 1:1 + size_x, 1:1 + size_y, :]
        result.append(center * (source_fluid * source + (1.0 - source_fluid) * own))
    return jnp.stack(result), center


def reference(populations, fluid_mask):
    fluid = fluid_mask.astype(jnp.float32)
    padded_fluid = jnp.pad(fluid, ((1, 1), (1, 1), (0, 0)))
    current = populations
    for step in range(STEPS):
        density, flux_x, flux_y, flux_z = moments(current)
        forcing = GAIN_RATE * (TARGET_SPEED - jnp.sum(fluid * flux_y) / jnp.sum(fluid * density))
        post = collide(current, fluid, forcing)
        post = jnp.pad(post, ((0, 0), (1, 1), (1, 1), (0, 0)))
        current, center = stream(post, padded_fluid)
    return current
```

```python
import jax
import jax.numpy as jnp
from jax import lax
from jax.experimental import pallas as pl
from jax.experimental.pallas import tpu as pltpu
from jax.sharding import Mesh
from jax.sharding import PartitionSpec as P

VELOCITIES = (
    (0, 0, 0),
    (1, 0, 0),
    (-1, 0, 0),
    (0, 1, 0),
    (0, -1, 0),
    (0, 0, 1),
    (0, 0, -1),
    (1, 1, 0),
    (-1, -1, 0),
    (1, -1, 0),
    (-1, 1, 0),
    (1, 0, 1),
    (-1, 0, -1),
    (1, 0, -1),
    (-1, 0, 1),
    (0, 1, 1),
    (0, -1, -1),
    (0, 1, -1),
    (0, -1, 1),
)
RELAX = 0.8
GAIN_RATE = 2.0
TARGET_SPEED = 0.05
KEEP = 1.0 / RELAX - 1.0

NX = 4
NY = 16
LANES = 128
ROWS = NY + 4
FRONT = 8
SOLID = 1e30
LIMIT = 1e29


def opposite_of(number):
    if number == 0:
        return 0
    return number + 1 if number % 2 == 1 else number - 1


def moments(f):
    total = [None] + [f[k] + f[k + 1] for k in range(1, 19, 2)]
    diff = [None] + [f[k] - f[k + 1] for k in range(1, 19, 2)]
    density = f[0]
    for value in total[1:]:
        density = density + value
    flux_x = diff[1] + diff[4] + diff[5] + diff[6] + diff[7]
    flux_y = diff[2] + (diff[4] - diff[5]) + (diff[8] + diff[9])
    flux_z = diff[3] + (diff[6] - diff[7]) + (diff[8] - diff[9])
    return density, flux_x, flux_y, flux_z, total, diff


def collide(f, fluid, shift):
    density, flux_x, flux_y, flux_z, total, diff = moments(f)
    inverse = 1.0 / (density + (1.0 - fluid))
    inverse = inverse * 1.5
    ux = flux_x * inverse
    uy = flux_y * inverse + 1.5 * shift
    uz = flux_z * inverse
    square = ux * ux + uy * uy + uz * uz
    base = 1.0 - square * (2.0 / 3.0)
    scaled = density * (1.0 / RELAX)
    open_site = fluid > 0.5
    weight = (scaled * (1.0 / 3.0), scaled * (1.0 / 18.0), scaled * (1.0 / 36.0))
    base_1 = weight[1] * base
    base_2 = weight[2] * base
    twice_1 = weight[1] * 2.0
    twice_2 = weight[2] * 2.0
    post = [jnp.where(open_site, weight[0] * base - KEEP * f[0], SOLID)]
    along = (None, ux, uy, uz, ux + uy, ux - uy, ux + uz, ux - uz, uy + uz, uy - uz)
    for pair in range(1, 10):
        speed = along[pair]
        odd = speed * (twice_1 if pair <= 3 else twice_2)
        even = (base_1 if pair <= 3 else base_2) + odd * speed
        even = even - (0.5 * KEEP) * total[pair]
        odd = odd - (0.5 * KEEP) * diff[pair]
        post.append(jnp.where(open_site, even + odd, SOLID))
        post.append(jnp.where(open_site, even - odd, SOLID))
    return post


def response(numbers, f, fluid):
    density, flux_x, flux_y, flux_z, _, _ = moments(f)
    inverse = 1.0 / (density + (1.0 - fluid))
    ux = flux_x * inverse
    uy = flux_y * inverse
    uz = flux_z * inverse
    base = 1.0 - 1.5 * (ux * ux + uy * uy + uz * uz)
    scaled = density * (fluid * (1.0 / RELAX))
    result = {}
    for number in numbers:
        move_x, move_y, move_z = VELOCITIES[number]
        weight = scaled * (1.0 / 18.0 if number < 7 else 1.0 / 36.0)
        speed = move_y * uy
        if move_x:
            speed = speed + move_x * ux
        if move_z:
            speed = speed + move_z * uz
        zero = weight * (base + speed * (3.0 + 4.5 * speed)) - (KEEP * fluid) * f[number]
        one = weight * (3.0 * move_y + 9.0 * move_y * speed - 3.0 * uy)
        two = weight * 3.0
        result[number] = (zero, one, two)
    return density, flux_y, result


def pack_kernel(pops, mask, to_low_y, to_high_y, to_low_x, to_high_x):
    for x in range(NX):
        for number in range(19):
            to_low_y[number, 2 * x : 2 * x + 2, :] = pops[number, x, 0:2, :]
            to_high_y[number, 2 * x : 2 * x + 2, :] = pops[number, x, NY - 2 : NY, :]
        to_low_y[19, 2 * x : 2 * x + 2, :] = mask[x, 0:2, :].astype(jnp.float32)
        to_high_y[19, 2 * x : 2 * x + 2, :] = mask[x, NY - 2 : NY, :].astype(jnp.float32)
    for out, x, up, down in ((to_low_x, 0, 10, 8), (to_high_x, NX - 1, 7, 9)):
        out[0:NY, :] = mask[x].astype(jnp.float32)
        out[NY : NY + 8, :] = jnp.zeros((8, 2 * LANES), jnp.float32)
        for place, y, number in ((0, NY - 1, up), (3, 0, down)):
            f = [pops[k, x, y : y + 1, :] for k in range(19)]
            fluid = mask[x, y : y + 1, :].astype(jnp.float32)
            _, _, coefs = response((number,), f, fluid)
            for i in range(3):
                row = NY + place + i
                out[row : row + 1, :] = coefs[number][i]


def sums_kernel(pops, mask, low_y, high_y, low_x, high_x, sums, to_low_x, to_high_x, flags):
    halves = (slice(0, LANES), slice(LANES, 2 * LANES))
    for out, first in ((to_low_x, 0), (to_high_x, NX - 2)):
        for layer in range(2):
            x = first + layer
            row = layer * ROWS
            for number in range(20):
                for half, lanes in enumerate(halves):
                    out[number, half, row : row + 2, :] = low_y[number, 2 * x : 2 * x + 2, lanes]
                    if number < 19:
                        out[number, half, row + 2 : row + 2 + NY, :] = pops[number, x, :, lanes]
                    else:
                        out[number, half, row + 2 : row + 2 + NY, :] = mask[x, :, lanes].astype(
                            jnp.float32
                        )
                    out[number, half, row + 2 + NY : row + ROWS, :] = high_y[
                        number, 2 * x : 2 * x + 2, lanes
                    ]
    flags[...] = jnp.zeros_like(flags)
    for half, lanes in enumerate(halves):
        for x in range(NX):
            row = FRONT + (x + 1) * ROWS
            flags[half, row + 1 : row + 2, :] = low_y[19, 2 * x + 1 : 2 * x + 2, lanes]
            flags[half, row + 2 : row + 2 + NY, :] = mask[x, :, lanes].astype(jnp.float32)
            flags[half, row + 2 + NY : row + 3 + NY, :] = high_y[19, 2 * x : 2 * x + 1, lanes]
        flags[half, FRONT + 2 : FRONT + 2 + NY, :] = low_x[0:NY, lanes]
        row = FRONT + (NX + 1) * ROWS
        flags[half, row + 2 : row + 2 + NY, :] = high_x[0:NY, lanes]
    lane = lax.broadcasted_iota(jnp.int32, (8, LANES), 1)
    numbers = [k for k in range(19) if VELOCITIES[k][1] != 0]
    acc = [jnp.zeros((8, LANES), jnp.float32) for _ in range(5)]
    for x in range(NX):
        for tile in range(NY // 8):
            row = FRONT + (x + 1) * ROWS + 2 + 8 * tile
            for half, lanes in enumerate(halves):
                f = [pops[k, x, 8 * tile : 8 * tile + 8, lanes] for k in range(19)]
                fluid = flags[half, row : row + 8, :]
                density, flux_y, coefs = response(numbers, f, fluid)
                acc[0] = acc[0] + fluid * flux_y
                acc[1] = acc[1] + fluid * density
                for number in numbers:
                    move_x, move_y, move_z = VELOCITIES[number]
                    start = row + move_x * ROWS + move_y
                    if move_z == 0:
                        ahead = flags[half, start : start + 8, :]
                    elif move_z == 1:
                        here = pltpu.roll(flags[half, start : start + 8, :], LANES - 1, 1)
                        if half == 0:
                            other = pltpu.roll(flags[1, start : start + 8, :], LANES - 1, 1)
                            ahead = jnp.where(lane == LANES - 1, other, here)
                        else:
                            ahead = jnp.where(lane == LANES - 1, 0.0, here)
                    else:
                        here = pltpu.roll(flags[half, start : start + 8, :], 1, 1)
                        if half == 1:
                            other = pltpu.roll(flags[0, start : start + 8, :], 1, 1)
                            ahead = jnp.where(lane == 0, other, here)
                        else:
                            ahead = jnp.where(lane == 0, 0.0, here)
                    sign = (2.0 * move_y) * ahead - move_y
                    for i in range(3):
                        acc[2 + i] = acc[2 + i] + sign * coefs[number][i]
    edge = [jnp.zeros((1, 2 * LANES), jnp.float32) for _ in range(3)]
    for beside, x in ((low_x, 0), (high_x, NX - 1)):
        for place, sign, flag in (
            (0, 2.0, high_y[19, 2 * x : 2 * x + 1, :]),
            (3, -2.0, low_y[19, 2 * x + 1 : 2 * x + 2, :]),
        ):
            for i in range(3):
                row = NY + place + i
                edge[i] = edge[i] + (sign * flag) * beside[row : row + 1, :]
    lane = lax.broadcasted_iota(jnp.int32, (1, LANES), 1)
    line = jnp.zeros((1, LANES), jnp.float32)
    for i in range(5):
        value = jnp.sum(acc[i], axis=0, keepdims=True)
        if i >= 2:
            value = value + (edge[i - 2][:, :LANES] + edge[i - 2][:, LANES:])
        value = jnp.sum(value, axis=1, keepdims=True)
        line = jnp.where(lane == i, value, line)
    sums[...] = jnp.broadcast_to(line[None], sums.shape)


def relay_kernel(arrived, sums):
    sums[...] = jnp.broadcast_to(jnp.sum(arrived[...], axis=0, keepdims=True), sums.shape)


def gather_row(post, number, half, row):
    return post[number, half, row : row + 8, :]


def streamed(post, row, lane):
    result = [[None] * 19, [None] * 19]
    for number in range(19):
        move_x, move_y, move_z = VELOCITIES[number]
        start = row - move_x * ROWS - move_y
        if number == 0:
            for half in range(2):
                result[half][0] = gather_row(post, 0, half, row)
            continue
        first = gather_row(post, number, 0, start)
        second = gather_row(post, number, 1, start)
        if move_z == 1:
            first = pltpu.roll(first, 1, 1)
            second = pltpu.roll(second, 1, 1)
            second = jnp.where(lane == 0, first, second)
            first = jnp.where(lane == 0, SOLID, first)
        elif move_z == -1:
            first = pltpu.roll(first, LANES - 1, 1)
            second = pltpu.roll(second, LANES - 1, 1)
            first = jnp.where(lane == LANES - 1, second, first)
            second = jnp.where(lane == LANES - 1, SOLID, second)
        for half, value in enumerate((first, second)):
            own = gather_row(post, opposite_of(number), half, row)
            result[half][number] = jnp.where(value < LIMIT, value, own)
    return result


def steps_kernel(arrived, pops, mask, low_y, high_y, low_x, high_x, out, post, later, flags):
    halves = (slice(0, LANES), slice(LANES, 2 * LANES))
    sums = jnp.sum(arrived[...], axis=0)

    def total(i):
        return jnp.broadcast_to(sums[:, i : i + 1], (8, LANES))

    mass = total(1)
    drive = GAIN_RATE * (TARGET_SPEED - total(0) / mass)
    shift_1 = RELAX * drive
    momentum = total(2) + shift_1 * (total(3) + shift_1 * total(4))
    drive = GAIN_RATE * (TARGET_SPEED - momentum / mass)
    shift_2 = RELAX * drive
    lane = lax.broadcasted_iota(jnp.int32, (8, LANES), 1)

    for x in range(NX):
        for tile in range(NY // 8):
            row = FRONT + (x + 2) * ROWS + 2 + 8 * tile
            for half, lanes in enumerate(halves):
                f = [pops[k, x, 8 * tile : 8 * tile + 8, lanes] for k in range(19)]
                fluid = mask[x, 8 * tile : 8 * tile + 8, lanes].astype(jnp.float32)
                flags[half, row : row + 8, :] = fluid
                for number, value in enumerate(collide(f, fluid, shift_1)):
                    post[number, half, row : row + 8, :] = value
    for beside, start in ((low_y, 0), (high_y, 2 + NY)):
        for half, lanes in enumerate(halves):
            f = [beside[k, :, lanes] for k in range(19)]
            fluid = beside[19, :, lanes]
            value = collide(f, fluid, shift_1)
            for x in range(NX):
                row = FRONT + (x + 2) * ROWS + start
                flags[half, row : row + 2, :] = fluid[2 * x : 2 * x + 2]
                for number in range(19):
                    post[number, half, row : row + 2, :] = value[number][2 * x : 2 * x + 2]
    for beside, start in ((low_x, 0), (high_x, (NX + 2) * ROWS)):
        for half in range(2):
            for tile in range(2 * ROWS // 8):
                at = slice(8 * tile, 8 * tile + 8)
                row = FRONT + start + 8 * tile
                f = [beside[k, half, at, :] for k in range(19)]
                fluid = beside[19, half, at, :]
                flags[half, row : row + 8, :] = fluid
                for number, value in enumerate(collide(f, fluid, shift_1)):
                    post[number, half, row : row + 8, :] = value
    for tile in range((NX + 2) * ROWS // 8):
        row = FRONT + ROWS + 8 * tile
        f = streamed(post, row, lane)
        for half in range(2):
            fluid = flags[half, row : row + 8, :]
            for number, value in enumerate(collide(f[half], fluid, shift_2)):
                later[number, half, row : row + 8, :] = value
    for x in range(NX):
        for tile in range(NY // 8):
            row = FRONT + (x + 2) * ROWS + 2 + 8 * tile
            f = streamed(later, row, lane)
            for half, lanes in enumerate(halves):
                open_site = flags[half, row : row + 8, :] > 0.5
                for number in range(19):
                    out[number, x, 8 * tile : 8 * tile + 8, lanes] = jnp.where(
                        open_site, f[half][number], 0.0
                    )


def f32(*shape):
    return jax.ShapeDtypeStruct(shape, jnp.float32)


def params():
    return pltpu.CompilerParams(vmem_limit_bytes=32 * 1024 * 1024)


def solution(mesh):
    regions, blocks = mesh.devices.shape
    cores = 2
    ring = 8 if blocks % 16 == 0 else 1
    grid = Mesh(
        mesh.devices.reshape(regions, blocks // (cores * ring), ring, cores),
        ("region", "x", "y", "core"),
    )
    local = ("x", "y", "core")
    first, second = regions * cores, blocks // cores

    def shifted(value, axis, count, step):
        pairs = [(i, i + step) for i in range(count) if 0 <= i + step < count]
        return lax.ppermute(value, axis, pairs)

    def on_device(pops, mask):
        to_low_y, to_high_y, to_low_x, to_high_x = pl.pallas_call(
            pack_kernel,
            out_shape=(f32(20, 8, 256), f32(20, 8, 256), f32(24, 256), f32(24, 256)),
            compiler_params=params(),
        )(pops, mask)
        low_y = shifted(to_high_y, "region", regions, 1)
        high_y = shifted(to_low_y, "region", regions, -1)
        low_x = shifted(to_high_x, local, blocks, 1)
        high_x = shifted(to_low_x, local, blocks, -1)
        sums, to_low_x, to_high_x = pl.pallas_call(
            sums_kernel,
            out_shape=(
                f32(first, 1, LANES),
                f32(20, 2, 2 * ROWS, LANES),
                f32(20, 2, 2 * ROWS, LANES),
            ),
            scratch_shapes=[pltpu.VMEM((2, FRONT + (NX + 2) * ROWS + 8, LANES), jnp.float32)],
            compiler_params=params(),
        )(pops, mask, low_y, high_y, low_x, high_x)
        low_x = shifted(to_high_x, local, blocks, 1)
        high_x = shifted(to_low_x, local, blocks, -1)
        sums = lax.all_to_all(sums, ("region", "core"), 0, 0, tiled=True)
        sums = pl.pallas_call(
            relay_kernel, out_shape=f32(second, 1, LANES), compiler_params=params()
        )(sums)
        sums = lax.all_to_all(sums, ("x", "y"), 0, 0, tiled=True)
        rows = FRONT + (NX + 4) * ROWS + 8
        return pl.pallas_call(
            steps_kernel,
            out_shape=f32(19, NX, NY, 2 * LANES),
            scratch_shapes=[
                pltpu.VMEM((19, 2, rows, LANES), jnp.float32),
                pltpu.VMEM((19, 2, rows, LANES), jnp.float32),
                pltpu.VMEM((2, rows, LANES), jnp.float32),
            ],
            compiler_params=params(),
        )(sums, pops, mask, low_y, high_y, low_x, high_x)

    return jax.shard_map(
        on_device,
        mesh=grid,
        in_specs=(P(None, local, "region", None), P(local, "region", None)),
        out_specs=P(None, local, "region", None),
        check_vma=False,
    )
```

```python
import jax
import jax.numpy as jnp
from jax import lax
from jax.experimental import pallas as pl
from jax.experimental.pallas import tpu as pltpu
from jax.sharding import Mesh
from jax.sharding import PartitionSpec as P

VELOCITIES = (
    (0, 0, 0),
    (1, 0, 0),
    (-1, 0, 0),
    (0, 1, 0),
    (0, -1, 0),
    (0, 0, 1),
    (0, 0, -1),
    (1, 1, 0),
    (-1, -1, 0),
    (1, -1, 0),
    (-1, 1, 0),
    (1, 0, 1),
    (-1, 0, -1),
    (1, 0, -1),
    (-1, 0, 1),
    (0, 1, 1),
    (0, -1, -1),
    (0, 1, -1),
    (0, -1, 1),
)
RELAX = 0.8
GAIN_RATE = 2.0
TARGET_SPEED = 0.05
KEEP = 1.0 / RELAX - 1.0

NX = 4
NY = 16
LANES = 128
ROWS = NY + 4
FRONT = 8
SOLID = 1e30
LIMIT = 1e29


def opposite_of(number):
    if number == 0:
        return 0
    return number + 1 if number % 2 == 1 else number - 1


def moments(f):
    total = [None] + [f[k] + f[k + 1] for k in range(1, 19, 2)]
    diff = [None] + [f[k] - f[k + 1] for k in range(1, 19, 2)]
    density = f[0]
    for value in total[1:]:
        density = density + value
    flux_x = diff[1] + diff[4] + diff[5] + diff[6] + diff[7]
    flux_y = diff[2] + (diff[4] - diff[5]) + (diff[8] + diff[9])
    flux_z = diff[3] + (diff[6] - diff[7]) + (diff[8] - diff[9])
    return density, flux_x, flux_y, flux_z, total, diff


def collide(f, fluid, shift):
    density, flux_x, flux_y, flux_z, total, diff = moments(f)
    inverse = 1.0 / (density + (1.0 - fluid))
    inverse = inverse * 1.5
    ux = flux_x * inverse
    uy = flux_y * inverse + 1.5 * shift
    uz = flux_z * inverse
    square = ux * ux + uy * uy + uz * uz
    base = 1.0 - square * (2.0 / 3.0)
    scaled = density * (1.0 / RELAX)
    open_site = fluid > 0.5
    weight = (scaled * (1.0 / 3.0), scaled * (1.0 / 18.0), scaled * (1.0 / 36.0))
    base_1 = weight[1] * base
    base_2 = weight[2] * base
    twice_1 = weight[1] * 2.0
    twice_2 = weight[2] * 2.0
    post = [jnp.where(open_site, weight[0] * base - KEEP * f[0], SOLID)]
    along = (None, ux, uy, uz, ux + uy, ux - uy, ux + uz, ux - uz, uy + uz, uy - uz)
    for pair in range(1, 10):
        speed = along[pair]
        odd = speed * (twice_1 if pair <= 3 else twice_2)
        even = (base_1 if pair <= 3 else base_2) + odd * speed
        even = even - (0.5 * KEEP) * total[pair]
        odd = odd - (0.5 * KEEP) * diff[pair]
        post.append(jnp.where(open_site, even + odd, SOLID))
        post.append(jnp.where(open_site, even - odd, SOLID))
    return post


def response(numbers, f, fluid):
    density, flux_x, flux_y, flux_z, _, _ = moments(f)
    inverse = 1.0 / (density + (1.0 - fluid))
    ux = flux_x * inverse
    uy = flux_y * inverse
    uz = flux_z * inverse
    base = 1.0 - 1.5 * (ux * ux + uy * uy + uz * uz)
    scaled = density * (fluid * (1.0 / RELAX))
    result = {}
    for number in numbers:
        move_x, move_y, move_z = VELOCITIES[number]
        weight = scaled * (1.0 / 18.0 if number < 7 else 1.0 / 36.0)
        speed = move_y * uy
        if move_x:
            speed = speed + move_x * ux
        if move_z:
            speed = speed + move_z * uz
        zero = weight * (base + speed * (3.0 + 4.5 * speed)) - (KEEP * fluid) * f[number]
        one = weight * (3.0 * move_y + 9.0 * move_y * speed - 3.0 * uy)
        two = weight * 3.0
        result[number] = (zero, one, two)
    return density, flux_y, result


def pack_kernel(pops, mask, to_low_y, to_high_y, to_low_x, to_high_x):
    for x in range(NX):
        for number in range(19):
            to_low_y[number, 2 * x : 2 * x + 2, :] = pops[number, x, 0:2, :]
            to_high_y[number, 2 * x : 2 * x + 2, :] = pops[number, x, NY - 2 : NY, :]
        to_low_y[19, 2 * x : 2 * x + 2, :] = mask[x, 0:2, :].astype(jnp.float32)
        to_high_y[19, 2 * x : 2 * x + 2, :] = mask[x, NY - 2 : NY, :].astype(jnp.float32)
    for out, x, up, down in ((to_low_x, 0, 10, 8), (to_high_x, NX - 1, 7, 9)):
        out[0:NY, :] = mask[x].astype(jnp.float32)
        out[NY : NY + 8, :] = jnp.zeros((8, 2 * LANES), jnp.float32)
        for place, y, number in ((0, NY - 1, up), (3, 0, down)):
            f = [pops[k, x, y : y + 1, :] for k in range(19)]
            fluid = mask[x, y : y + 1, :].astype(jnp.float32)
            _, _, coefs = response((number,), f, fluid)
            for i in range(3):
                row = NY + place + i
                out[row : row + 1, :] = coefs[number][i]


def sums_kernel(pops, mask, low_y, high_y, low_x, high_x, sums, to_low_x, to_high_x, flags):
    halves = (slice(0, LANES), slice(LANES, 2 * LANES))
    for out, first in ((to_low_x, 0), (to_high_x, NX - 2)):
        for layer in range(2):
            x = first + layer
            row = layer * ROWS
            for number in range(20):
                for half, lanes in enumerate(halves):
                    out[number, half, row : row + 2, :] = low_y[number, 2 * x : 2 * x + 2, lanes]
                    if number < 19:
                        out[number, half, row + 2 : row + 2 + NY, :] = pops[number, x, :, lanes]
                    else:
                        out[number, half, row + 2 : row + 2 + NY, :] = mask[x, :, lanes].astype(
                            jnp.float32
                        )
                    out[number, half, row + 2 + NY : row + ROWS, :] = high_y[
                        number, 2 * x : 2 * x + 2, lanes
                    ]
    flags[...] = jnp.zeros_like(flags)
    for half, lanes in enumerate(halves):
        for x in range(NX):
            row = FRONT + (x + 1) * ROWS
            flags[half, row + 1 : row + 2, :] = low_y[19, 2 * x + 1 : 2 * x + 2, lanes]
            flags[half, row + 2 : row + 2 + NY, :] = mask[x, :, lanes].astype(jnp.float32)
            flags[half, row + 2 + NY : row + 3 + NY, :] = high_y[19, 2 * x : 2 * x + 1, lanes]
        flags[half, FRONT + 2 : FRONT + 2 + NY, :] = low_x[0:NY, lanes]
        row = FRONT + (NX + 1) * ROWS
        flags[half, row + 2 : row + 2 + NY, :] = high_x[0:NY, lanes]
    lane = lax.broadcasted_iota(jnp.int32, (8, LANES), 1)
    numbers = [k for k in range(19) if VELOCITIES[k][1] != 0]
    acc = [jnp.zeros((8, LANES), jnp.float32) for _ in range(5)]
    for x in range(NX):
        for tile in range(NY // 8):
            row = FRONT + (x + 1) * ROWS + 2 + 8 * tile
            for half, lanes in enumerate(halves):
                f = [pops[k, x, 8 * tile : 8 * tile + 8, lanes] for k in range(19)]
                fluid = flags[half, row : row + 8, :]
                density, flux_y, coefs = response(numbers, f, fluid)
                acc[0] = acc[0] + fluid * flux_y
                acc[1] = acc[1] + fluid * density
                for number in numbers:
                    move_x, move_y, move_z = VELOCITIES[number]
                    start = row + move_x * ROWS + move_y
                    if move_z == 0:
                        ahead = flags[half, start : start + 8, :]
                    elif move_z == 1:
                        here = pltpu.roll(flags[half, start : start + 8, :], LANES - 1, 1)
                        if half == 0:
                            other = pltpu.roll(flags[1, start : start + 8, :], LANES - 1, 1)
                            ahead = jnp.where(lane == LANES - 1, other, here)
                        else:
                            ahead = jnp.where(lane == LANES - 1, 0.0, here)
                    else:
                        here = pltpu.roll(flags[half, start : start + 8, :], 1, 1)
                        if half == 1:
                            other = pltpu.roll(flags[0, start : start + 8, :], 1, 1)
                            ahead = jnp.where(lane == 0, other, here)
                        else:
                            ahead = jnp.where(lane == 0, 0.0, here)
                    sign = (2.0 * move_y) * ahead - move_y
                    for i in range(3):
                        acc[2 + i] = acc[2 + i] + sign * coefs[number][i]
    edge = [jnp.zeros((1, 2 * LANES), jnp.float32) for _ in range(3)]
    for beside, x in ((low_x, 0), (high_x, NX - 1)):
        for place, sign, flag in (
            (0, 2.0, high_y[19, 2 * x : 2 * x + 1, :]),
            (3, -2.0, low_y[19, 2 * x + 1 : 2 * x + 2, :]),
        ):
            for i in range(3):
                row = NY + place + i
                edge[i] = edge[i] + (sign * flag) * beside[row : row + 1, :]
    lane = lax.broadcasted_iota(jnp.int32, (1, LANES), 1)
    line = jnp.zeros((1, LANES), jnp.float32)
    for i in range(5):
        value = jnp.sum(acc[i], axis=0, keepdims=True)
        if i >= 2:
            value = value + (edge[i - 2][:, :LANES] + edge[i - 2][:, LANES:])
        value = jnp.sum(value, axis=1, keepdims=True)
        line = jnp.where(lane == i, value, line)
    sums[...] = jnp.broadcast_to(line[None], sums.shape)


def relay_kernel(arrived, sums):
    sums[...] = jnp.broadcast_to(jnp.sum(arrived[...], axis=0, keepdims=True), sums.shape)


def gather_row(post, number, half, row):
    return post[number, half, row : row + 8, :]


def streamed(post, row, lane):
    result = [[None] * 19, [None] * 19]
    for number in range(19):
        move_x, move_y, move_z = VELOCITIES[number]
        start = row - move_x * ROWS - move_y
        if number == 0:
            for half in range(2):
                result[half][0] = gather_row(post, 0, half, row)
            continue
        first = gather_row(post, number, 0, start)
        second = gather_row(post, number, 1, start)
        if move_z == 1:
            first = pltpu.roll(first, 1, 1)
            second = pltpu.roll(second, 1, 1)
            second = jnp.where(lane == 0, first, second)
            first = jnp.where(lane == 0, SOLID, first)
        elif move_z == -1:
            first = pltpu.roll(first, LANES - 1, 1)
            second = pltpu.roll(second, LANES - 1, 1)
            first = jnp.where(lane == LANES - 1, second, first)
            second = jnp.where(lane == LANES - 1, SOLID, second)
        for half, value in enumerate((first, second)):
            own = gather_row(post, opposite_of(number), half, row)
            result[half][number] = jnp.where(value < LIMIT, value, own)
    return result


def steps_kernel(arrived, pops, mask, low_y, high_y, low_x, high_x, out, post, later, flags):
    halves = (slice(0, LANES), slice(LANES, 2 * LANES))
    sums = jnp.sum(arrived[...], axis=0)

    def total(i):
        return jnp.broadcast_to(sums[:, i : i + 1], (8, LANES))

    mass = total(1)
    drive = GAIN_RATE * (TARGET_SPEED - total(0) / mass)
    shift_1 = RELAX * drive
    momentum = total(2) + shift_1 * (total(3) + shift_1 * total(4))
    drive = GAIN_RATE * (TARGET_SPEED - momentum / mass)
    shift_2 = RELAX * drive
    lane = lax.broadcasted_iota(jnp.int32, (8, LANES), 1)

    for x in range(NX):
        for tile in range(NY // 8):
            row = FRONT + (x + 2) * ROWS + 2 + 8 * tile
            for half, lanes in enumerate(halves):
                f = [pops[k, x, 8 * tile : 8 * tile + 8, lanes] for k in range(19)]
                fluid = mask[x, 8 * tile : 8 * tile + 8, lanes].astype(jnp.float32)
                flags[half, row : row + 8, :] = fluid
                for number, value in enumerate(collide(f, fluid, shift_1)):
                    post[number, half, row : row + 8, :] = value
    for beside, start in ((low_y, 0), (high_y, 2 + NY)):
        for half, lanes in enumerate(halves):
            f = [beside[k, :, lanes] for k in range(19)]
            fluid = beside[19, :, lanes]
            value = collide(f, fluid, shift_1)
            for x in range(NX):
                row = FRONT + (x + 2) * ROWS + start
                flags[half, row : row + 2, :] = fluid[2 * x : 2 * x + 2]
                for number in range(19):
                    post[number, half, row : row + 2, :] = value[number][2 * x : 2 * x + 2]
    for beside, start in ((low_x, 0), (high_x, (NX + 2) * ROWS)):
        for half in range(2):
            for tile in range(2 * ROWS // 8):
                at = slice(8 * tile, 8 * tile + 8)
                row = FRONT + start + 8 * tile
                f = [beside[k, half, at, :] for k in range(19)]
                fluid = beside[19, half, at, :]
                flags[half, row : row + 8, :] = fluid
                for number, value in enumerate(collide(f, fluid, shift_1)):
                    post[number, half, row : row + 8, :] = value
    for tile in range((NX + 2) * ROWS // 8):
        row = FRONT + ROWS + 8 * tile
        f = streamed(post, row, lane)
        for half in range(2):
            fluid = flags[half, row : row + 8, :]
            for number, value in enumerate(collide(f[half], fluid, shift_2)):
                later[number, half, row : row + 8, :] = value
    for x in range(NX):
        for tile in range(NY // 8):
            row = FRONT + (x + 2) * ROWS + 2 + 8 * tile
            f = streamed(later, row, lane)
            for half, lanes in enumerate(halves):
                open_site = flags[half, row : row + 8, :] > 0.5
                for number in range(19):
                    out[number, x, 8 * tile : 8 * tile + 8, lanes] = jnp.where(
                        open_site, f[half][number], 0.0
                    )


def f32(*shape):
    return jax.ShapeDtypeStruct(shape, jnp.float32)


def params():
    return pltpu.CompilerParams(vmem_limit_bytes=32 * 1024 * 1024)


def solution(mesh):
    regions, blocks = mesh.devices.shape
    cores = 2
    ring = 8 if blocks % 16 == 0 else 1
    grid = Mesh(
        mesh.devices.reshape(regions, blocks // (cores * ring), ring, cores),
        ("region", "x", "y", "core"),
    )
    local = ("x", "y", "core")
    first, second = blocks // cores, regions * cores

    def shifted(value, axis, count, step):
        pairs = [(i, i + step) for i in range(count) if 0 <= i + step < count]
        return lax.ppermute(value, axis, pairs)

    def on_device(pops, mask):
        to_low_y, to_high_y, to_low_x, to_high_x = pl.pallas_call(
            pack_kernel,
            out_shape=(f32(20, 8, 256), f32(20, 8, 256), f32(24, 256), f32(24, 256)),
            compiler_params=params(),
        )(pops, mask)
        low_y = shifted(to_high_y, "region", regions, 1)
        high_y = shifted(to_low_y, "region", regions, -1)
        low_x = shifted(to_high_x, local, blocks, 1)
        high_x = shifted(to_low_x, local, blocks, -1)
        sums, to_low_x, to_high_x = pl.pallas_call(
            sums_kernel,
            out_shape=(
                f32(first, 1, LANES),
                f32(20, 2, 2 * ROWS, LANES),
                f32(20, 2, 2 * ROWS, LANES),
            ),
            scratch_shapes=[pltpu.VMEM((2, FRONT + (NX + 2) * ROWS + 8, LANES), jnp.float32)],
            compiler_params=params(),
        )(pops, mask, low_y, high_y, low_x, high_x)
        low_x = shifted(to_high_x, local, blocks, 1)
        high_x = shifted(to_low_x, local, blocks, -1)
        sums = lax.all_to_all(sums, ("x", "y"), 0, 0, tiled=True)
        sums = pl.pallas_call(
            relay_kernel, out_shape=f32(second, 1, LANES), compiler_params=params()
        )(sums)
        sums = lax.all_to_all(sums, ("region", "core"), 0, 0, tiled=True)
        rows = FRONT + (NX + 4) * ROWS + 8
        return pl.pallas_call(
            steps_kernel,
            out_shape=f32(19, NX, NY, 2 * LANES),
            scratch_shapes=[
                pltpu.VMEM((19, 2, rows, LANES), jnp.float32),
                pltpu.VMEM((19, 2, rows, LANES), jnp.float32),
                pltpu.VMEM((2, rows, LANES), jnp.float32),
            ],
            compiler_params=params(),
        )(sums, pops, mask, low_y, high_y, low_x, high_x)

    return jax.shard_map(
        on_device,
        mesh=grid,
        in_specs=(P(None, local, "region", None), P(local, "region", None)),
        out_specs=P(None, local, "region", None),
        check_vma=False,
    )
```

```python
import jax
import jax.numpy as jnp
from jax import lax
from jax.experimental import pallas as pl
from jax.experimental.pallas import tpu as pltpu
from jax.sharding import Mesh
from jax.sharding import PartitionSpec as P

VELOCITIES = (
    (0, 0, 0),
    (1, 0, 0),
    (-1, 0, 0),
    (0, 1, 0),
    (0, -1, 0),
    (0, 0, 1),
    (0, 0, -1),
    (1, 1, 0),
    (-1, -1, 0),
    (1, -1, 0),
    (-1, 1, 0),
    (1, 0, 1),
    (-1, 0, -1),
    (1, 0, -1),
    (-1, 0, 1),
    (0, 1, 1),
    (0, -1, -1),
    (0, 1, -1),
    (0, -1, 1),
)
RELAX = 0.8
GAIN_RATE = 2.0
TARGET_SPEED = 0.05
KEEP = 1.0 / RELAX - 1.0

NX = 4
NY = 16
LANES = 128
ROWS = NY + 4
FRONT = 8
SOLID = 1e30
LIMIT = 1e29


def opposite_of(number):
    if number == 0:
        return 0
    return number + 1 if number % 2 == 1 else number - 1


def moments(f):
    total = [None] + [f[k] + f[k + 1] for k in range(1, 19, 2)]
    diff = [None] + [f[k] - f[k + 1] for k in range(1, 19, 2)]
    density = f[0]
    for value in total[1:]:
        density = density + value
    flux_x = diff[1] + diff[4] + diff[5] + diff[6] + diff[7]
    flux_y = diff[2] + (diff[4] - diff[5]) + (diff[8] + diff[9])
    flux_z = diff[3] + (diff[6] - diff[7]) + (diff[8] - diff[9])
    return density, flux_x, flux_y, flux_z, total, diff


def collide(f, fluid, shift):
    density, flux_x, flux_y, flux_z, total, diff = moments(f)
    inverse = 1.0 / (density + (1.0 - fluid))
    inverse = inverse * 1.5
    ux = flux_x * inverse
    uy = flux_y * inverse + 1.5 * shift
    uz = flux_z * inverse
    square = ux * ux + uy * uy + uz * uz
    base = 1.0 - square * (2.0 / 3.0)
    scaled = density * (1.0 / RELAX)
    open_site = fluid > 0.5
    weight = (scaled * (1.0 / 3.0), scaled * (1.0 / 18.0), scaled * (1.0 / 36.0))
    base_1 = weight[1] * base
    base_2 = weight[2] * base
    twice_1 = weight[1] * 2.0
    twice_2 = weight[2] * 2.0
    post = [jnp.where(open_site, weight[0] * base - KEEP * f[0], SOLID)]
    along = (None, ux, uy, uz, ux + uy, ux - uy, ux + uz, ux - uz, uy + uz, uy - uz)
    for pair in range(1, 10):
        speed = along[pair]
        odd = speed * (twice_1 if pair <= 3 else twice_2)
        even = (base_1 if pair <= 3 else base_2) + odd * speed
        even = even - (0.5 * KEEP) * total[pair]
        odd = odd - (0.5 * KEEP) * diff[pair]
        post.append(jnp.where(open_site, even + odd, SOLID))
        post.append(jnp.where(open_site, even - odd, SOLID))
    return post


def response(numbers, f, fluid):
    density, flux_x, flux_y, flux_z, _, _ = moments(f)
    inverse = 1.0 / (density + (1.0 - fluid))
    ux = flux_x * inverse
    uy = flux_y * inverse
    uz = flux_z * inverse
    base = 1.0 - 1.5 * (ux * ux + uy * uy + uz * uz)
    scaled = density * (fluid * (1.0 / RELAX))
    result = {}
    for number in numbers:
        move_x, move_y, move_z = VELOCITIES[number]
        weight = scaled * (1.0 / 18.0 if number < 7 else 1.0 / 36.0)
        speed = move_y * uy
        if move_x:
            speed = speed + move_x * ux
        if move_z:
            speed = speed + move_z * uz
        zero = weight * (base + speed * (3.0 + 4.5 * speed)) - (KEEP * fluid) * f[number]
        one = weight * (3.0 * move_y + 9.0 * move_y * speed - 3.0 * uy)
        two = weight * 3.0
        result[number] = (zero, one, two)
    return density, flux_y, result


def pack_kernel(pops, mask, to_low_y, to_high_y):
    for x in range(NX):
        rows = slice(2 * x, 2 * x + 2)
        for number in range(19):
            to_low_y[number, rows, :] = pops[number, x, 0:2, :]
            to_high_y[number, rows, :] = pops[number, x, NY - 2 : NY, :]
        to_low_y[19, rows, :] = mask[x, 0:2, :].astype(jnp.float32)
        to_high_y[19, rows, :] = mask[x, NY - 2 : NY, :].astype(jnp.float32)


def sums_kernel(pops, mask, low_y, high_y, mate_mask, far_mask, sums, to_mate, to_far, flags):
    halves = (slice(0, LANES), slice(LANES, 2 * LANES))
    core = lax.axis_index("core")
    def pack(out, first):
        for layer in range(2):
            x = first + layer
            row = layer * ROWS
            pair = slice(2 * x, 2 * x + 2)
            for number in range(20):
                for half, lanes in enumerate(halves):
                    out[number, half, row : row + 2, :] = low_y[number, pair, lanes]
                    if number < 19:
                        block = pops[number, x, :, lanes]
                    else:
                        block = mask[x, :, lanes].astype(jnp.float32)
                    out[number, half, row + 2 : row + 2 + NY, :] = block
                    out[number, half, row + 2 + NY : row + ROWS, :] = high_y[number, pair, lanes]

    @pl.when(core == 0)
    def _():
        pack(to_mate, NX - 2)
        pack(to_far, 0)

    @pl.when(core == 1)
    def _():
        pack(to_mate, 0)
        pack(to_far, NX - 2)

    first_core = core == 0
    low_x = jnp.where(first_core, far_mask[NX - 1], mate_mask[NX - 1]).astype(jnp.float32)
    high_x = jnp.where(first_core, mate_mask[0], far_mask[0]).astype(jnp.float32)
    flags[...] = jnp.zeros_like(flags)
    for half, lanes in enumerate(halves):
        for x in range(NX):
            row = FRONT + (x + 1) * ROWS
            flags[half, row + 1 : row + 2, :] = low_y[19, 2 * x + 1 : 2 * x + 2, lanes]
            flags[half, row + 2 : row + 2 + NY, :] = mask[x, :, lanes].astype(jnp.float32)
            flags[half, row + 2 + NY : row + 3 + NY, :] = high_y[19, 2 * x : 2 * x + 1, lanes]
        flags[half, FRONT + 2 : FRONT + 2 + NY, :] = low_x[:, lanes]
        row = FRONT + (NX + 1) * ROWS
        flags[half, row + 2 : row + 2 + NY, :] = high_x[:, lanes]
    lane = lax.broadcasted_iota(jnp.int32, (8, LANES), 1)
    numbers = [k for k in range(19) if VELOCITIES[k][1] != 0]
    acc = [jnp.zeros((8, LANES), jnp.float32) for _ in range(5)]
    for x in range(NX):
        for tile in range(NY // 8):
            row = FRONT + (x + 1) * ROWS + 2 + 8 * tile
            for half, lanes in enumerate(halves):
                f = [pops[k, x, 8 * tile : 8 * tile + 8, lanes] for k in range(19)]
                fluid = flags[half, row : row + 8, :]
                density, flux_y, coefs = response(numbers, f, fluid)
                acc[0] = acc[0] + fluid * flux_y
                acc[1] = acc[1] + fluid * density
                for number in numbers:
                    move_x, move_y, move_z = VELOCITIES[number]
                    start = row + move_x * ROWS + move_y
                    if move_z == 0:
                        ahead = flags[half, start : start + 8, :]
                    elif move_z == 1:
                        here = pltpu.roll(flags[half, start : start + 8, :], LANES - 1, 1)
                        if half == 0:
                            other = pltpu.roll(flags[1, start : start + 8, :], LANES - 1, 1)
                            ahead = jnp.where(lane == LANES - 1, other, here)
                        else:
                            ahead = jnp.where(lane == LANES - 1, 0.0, here)
                    else:
                        here = pltpu.roll(flags[half, start : start + 8, :], 1, 1)
                        if half == 1:
                            other = pltpu.roll(flags[0, start : start + 8, :], 1, 1)
                            ahead = jnp.where(lane == 0, other, here)
                        else:
                            ahead = jnp.where(lane == 0, 0.0, here)
                    sign = (2.0 * move_y) * ahead - move_y
                    for i in range(3):
                        acc[2 + i] = acc[2 + i] + sign * coefs[number][i]
    place = lax.broadcasted_iota(jnp.int32, (8, LANES), 0)
    for beside, y, sign, links in (
        (low_y, 0, 2.0, ((10, 1, low_x), (7, 2 * NX - 1, high_x))),
        (high_y, NY - 1, -2.0, ((8, 0, low_x), (9, 2 * NX - 2, high_x))),
    ):
        for lanes in halves:
            f = [beside[k, :, lanes] for k in range(19)]
            _, _, coefs = response([link[0] for link in links], f, beside[19, :, lanes])
            for number, row, layer in links:
                ahead = jnp.where(place == row, sign * layer[y : y + 1, lanes], 0.0)
                for i in range(3):
                    acc[2 + i] = acc[2 + i] + ahead * coefs[number][i]
    lane = lax.broadcasted_iota(jnp.int32, (1, LANES), 1)
    line = jnp.zeros((1, LANES), jnp.float32)
    for i in range(5):
        value = jnp.sum(acc[i], axis=0, keepdims=True)
        value = jnp.sum(value, axis=1, keepdims=True)
        line = jnp.where(lane == i, value, line)
    sums[...] = jnp.broadcast_to(line[None], sums.shape)


def relay_kernel(arrived, sums):
    sums[...] = jnp.broadcast_to(jnp.sum(arrived[...], axis=0, keepdims=True), sums.shape)


def gather_row(post, number, half, row):
    return post[number, half, row : row + 8, :]


def streamed(post, row, lane):
    result = [[None] * 19, [None] * 19]
    for number in range(19):
        move_x, move_y, move_z = VELOCITIES[number]
        start = row - move_x * ROWS - move_y
        if number == 0:
            for half in range(2):
                result[half][0] = gather_row(post, 0, half, row)
            continue
        first = gather_row(post, number, 0, start)
        second = gather_row(post, number, 1, start)
        if move_z == 1:
            first = pltpu.roll(first, 1, 1)
            second = pltpu.roll(second, 1, 1)
            second = jnp.where(lane == 0, first, second)
            first = jnp.where(lane == 0, SOLID, first)
        elif move_z == -1:
            first = pltpu.roll(first, LANES - 1, 1)
            second = pltpu.roll(second, LANES - 1, 1)
            first = jnp.where(lane == LANES - 1, second, first)
            second = jnp.where(lane == LANES - 1, SOLID, second)
        for half, value in enumerate((first, second)):
            own = gather_row(post, opposite_of(number), half, row)
            result[half][number] = jnp.where(value < LIMIT, value, own)
    return result


def steps_kernel(arrived, pops, mask, low_y, high_y, mate, far, out, post, later, flags):
    halves = (slice(0, LANES), slice(LANES, 2 * LANES))
    sums = jnp.sum(arrived[...], axis=0)

    def total(i):
        return jnp.broadcast_to(sums[:, i : i + 1], (8, LANES))

    mass = total(1)
    drive = GAIN_RATE * (TARGET_SPEED - total(0) / mass)
    shift_1 = RELAX * drive
    momentum = total(2) + shift_1 * (total(3) + shift_1 * total(4))
    drive = GAIN_RATE * (TARGET_SPEED - momentum / mass)
    shift_2 = RELAX * drive
    lane = lax.broadcasted_iota(jnp.int32, (8, LANES), 1)

    for x in range(NX):
        for tile in range(NY // 8):
            row = FRONT + (x + 2) * ROWS + 2 + 8 * tile
            for half, lanes in enumerate(halves):
                f = [pops[k, x, 8 * tile : 8 * tile + 8, lanes] for k in range(19)]
                fluid = mask[x, 8 * tile : 8 * tile + 8, lanes].astype(jnp.float32)
                flags[half, row : row + 8, :] = fluid
                for number, value in enumerate(collide(f, fluid, shift_1)):
                    post[number, half, row : row + 8, :] = value
    for beside, start in ((low_y, 0), (high_y, 2 + NY)):
        for half, lanes in enumerate(halves):
            f = [beside[k, :, lanes] for k in range(19)]
            fluid = beside[19, :, lanes]
            value = collide(f, fluid, shift_1)
            for x in range(NX):
                row = FRONT + (x + 2) * ROWS + start
                flags[half, row : row + 2, :] = fluid[2 * x : 2 * x + 2]
                for number in range(19):
                    post[number, half, row : row + 2, :] = value[number][2 * x : 2 * x + 2]
    core = lax.axis_index("core")
    for beside, side in ((mate, 1 - core), (far, core)):
        start = pl.multiple_of(FRONT + side * ((NX + 2) * ROWS), 8)
        for half in range(2):
            for tile in range(2 * ROWS // 8):
                at = slice(8 * tile, 8 * tile + 8)
                rows = pl.ds(start + 8 * tile, 8)
                f = [beside[k, half, at, :] for k in range(19)]
                fluid = beside[19, half, at, :]
                flags[half, rows, :] = fluid
                for number, value in enumerate(collide(f, fluid, shift_1)):
                    post[number, half, rows, :] = value
    for tile in range((NX + 2) * ROWS // 8):
        row = FRONT + ROWS + 8 * tile
        f = streamed(post, row, lane)
        for half in range(2):
            fluid = flags[half, row : row + 8, :]
            for number, value in enumerate(collide(f[half], fluid, shift_2)):
                later[number, half, row : row + 8, :] = value
    for x in range(NX):
        for tile in range(NY // 8):
            row = FRONT + (x + 2) * ROWS + 2 + 8 * tile
            f = streamed(later, row, lane)
            for half, lanes in enumerate(halves):
                open_site = flags[half, row : row + 8, :] > 0.5
                for number in range(19):
                    out[number, x, 8 * tile : 8 * tile + 8, lanes] = jnp.where(
                        open_site, f[half][number], 0.0
                    )


def f32(*shape):
    return jax.ShapeDtypeStruct(shape, jnp.float32)


def params():
    return pltpu.CompilerParams(vmem_limit_bytes=32 * 1024 * 1024)


def solution(mesh):
    regions, blocks = mesh.devices.shape
    cores = 2
    ring = 8 if blocks % 16 == 0 else 1
    grid = Mesh(
        mesh.devices.reshape(regions, blocks // (cores * ring), ring, cores),
        ("region", "x", "y", "core"),
    )
    local = ("x", "y", "core")
    first, second = blocks // cores, regions * cores

    def shifted(value, step):
        pairs = [(i, i + step) for i in range(regions) if 0 <= i + step < regions]
        return lax.ppermute(value, "region", pairs)

    def from_mate(value):
        return lax.ppermute(value, "core", [(0, 1), (1, 0)])

    def from_far(value):
        ends = [(i, i + 1) for i in range(1, blocks - 1, 2)]
        return lax.ppermute(value, local, ends + [(j, i) for i, j in ends])

    def on_device(pops, mask):
        mate_mask = from_mate(mask)
        to_low_y, to_high_y = pl.pallas_call(
            pack_kernel,
            out_shape=(f32(20, 8, 256), f32(20, 8, 256)),
            compiler_params=params(),
        )(pops, mask)
        low_y = shifted(to_high_y, 1)
        high_y = shifted(to_low_y, -1)
        far_mask = from_far(mask)
        sums, to_mate, to_far = pl.pallas_call(
            sums_kernel,
            out_shape=(
                f32(first, 1, LANES),
                f32(20, 2, 2 * ROWS, LANES),
                f32(20, 2, 2 * ROWS, LANES),
            ),
            scratch_shapes=[pltpu.VMEM((2, FRONT + (NX + 2) * ROWS + 8, LANES), jnp.float32)],
            compiler_params=params(),
        )(pops, mask, low_y, high_y, mate_mask, far_mask)
        mate = from_mate(to_mate)
        far = from_far(to_far)
        sums = lax.all_to_all(sums, ("x", "y"), 0, 0, tiled=True)
        sums = pl.pallas_call(
            relay_kernel, out_shape=f32(second, 1, LANES), compiler_params=params()
        )(sums)
        sums = lax.all_to_all(sums, ("region", "core"), 0, 0, tiled=True)
        rows = FRONT + (NX + 4) * ROWS + 8
        return pl.pallas_call(
            steps_kernel,
            out_shape=f32(19, NX, NY, 2 * LANES),
            scratch_shapes=[
                pltpu.VMEM((19, 2, rows, LANES), jnp.float32),
                pltpu.VMEM((19, 2, rows, LANES), jnp.float32),
                pltpu.VMEM((2, rows, LANES), jnp.float32),
            ],
            compiler_params=params(),
        )(sums, pops, mask, low_y, high_y, mate, far)

    return jax.shard_map(
        on_device,
        mesh=grid,
        in_specs=(P(None, local, "region", None), P(local, "region", None)),
        out_specs=P(None, local, "region", None),
        check_vma=False,
    )
```

```python
import jax
import jax.numpy as jnp
from jax import lax
from jax.experimental import pallas as pl
from jax.experimental.pallas import tpu as pltpu
from jax.sharding import Mesh
from jax.sharding import PartitionSpec as P

VELOCITIES = (
    (0, 0, 0),
    (1, 0, 0),
    (-1, 0, 0),
    (0, 1, 0),
    (0, -1, 0),
    (0, 0, 1),
    (0, 0, -1),
    (1, 1, 0),
    (-1, -1, 0),
    (1, -1, 0),
    (-1, 1, 0),
    (1, 0, 1),
    (-1, 0, -1),
    (1, 0, -1),
    (-1, 0, 1),
    (0, 1, 1),
    (0, -1, -1),
    (0, 1, -1),
    (0, -1, 1),
)
RELAX = 0.8
GAIN_RATE = 2.0
TARGET_SPEED = 0.05
KEEP = 1.0 / RELAX - 1.0

NX = 4
NY = 16
LANES = 128
ROWS = NY + 4
FRONT = 8
SOLID = 1e30
LIMIT = 1e29
HALVES = (slice(0, LANES), slice(LANES, 2 * LANES))
TOWARD_HIGH = (1, 7, 9, 11, 13)
TOWARD_LOW = (2, 10, 8, 14, 12)
SLOTS = 15


def opposite_of(number):
    if number == 0:
        return 0
    return number + 1 if number % 2 == 1 else number - 1


def moments(f):
    total = [None] + [f[k] + f[k + 1] for k in range(1, 19, 2)]
    diff = [None] + [f[k] - f[k + 1] for k in range(1, 19, 2)]
    density = f[0]
    for value in total[1:]:
        density = density + value
    flux_x = diff[1] + diff[4] + diff[5] + diff[6] + diff[7]
    flux_y = diff[2] + (diff[4] - diff[5]) + (diff[8] + diff[9])
    flux_z = diff[3] + (diff[6] - diff[7]) + (diff[8] - diff[9])
    return density, flux_x, flux_y, flux_z, total, diff


def collide(f, fluid, shift):
    density, flux_x, flux_y, flux_z, total, diff = moments(f)
    inverse = 1.0 / (density + (1.0 - fluid))
    inverse = inverse * 1.5
    ux = flux_x * inverse
    uy = flux_y * inverse + 1.5 * shift
    uz = flux_z * inverse
    square = ux * ux + uy * uy + uz * uz
    base = 1.0 - square * (2.0 / 3.0)
    scaled = density * (1.0 / RELAX)
    open_site = fluid > 0.5
    weight = (scaled * (1.0 / 3.0), scaled * (1.0 / 18.0), scaled * (1.0 / 36.0))
    base_1 = weight[1] * base
    base_2 = weight[2] * base
    twice_1 = weight[1] * 2.0
    twice_2 = weight[2] * 2.0
    post = [jnp.where(open_site, weight[0] * base - KEEP * f[0], SOLID)]
    along = (None, ux, uy, uz, ux + uy, ux - uy, ux + uz, ux - uz, uy + uz, uy - uz)
    for pair in range(1, 10):
        speed = along[pair]
        odd = speed * (twice_1 if pair <= 3 else twice_2)
        even = (base_1 if pair <= 3 else base_2) + odd * speed
        even = even - (0.5 * KEEP) * total[pair]
        odd = odd - (0.5 * KEEP) * diff[pair]
        post.append(jnp.where(open_site, even + odd, SOLID))
        post.append(jnp.where(open_site, even - odd, SOLID))
    return post


def response(numbers, f, fluid):
    density, flux_x, flux_y, flux_z, _, _ = moments(f)
    inverse = 1.0 / (density + (1.0 - fluid))
    ux = flux_x * inverse
    uy = flux_y * inverse
    uz = flux_z * inverse
    base = 1.0 - 1.5 * (ux * ux + uy * uy + uz * uz)
    scaled = density * (fluid * (1.0 / RELAX))
    result = {}
    for number in numbers:
        move_x, move_y, move_z = VELOCITIES[number]
        weight = scaled * (1.0 / 18.0 if number < 7 else 1.0 / 36.0)
        speed = move_y * uy
        if move_x:
            speed = speed + move_x * ux
        if move_z:
            speed = speed + move_z * uz
        zero = weight * (base + speed * (3.0 + 4.5 * speed)) - (KEEP * fluid) * f[number]
        one = weight * (3.0 * move_y + 9.0 * move_y * speed - 3.0 * uy)
        two = weight * 3.0
        result[number] = (zero, one, two)
    return density, flux_y, result


def pack_kernel(
    pops_in, mask_in, pops, mask, to_low_y, to_high_y, to_far, to_mate, pops_sem, mask_sem
):
    pops_copy = pltpu.make_async_copy(pops_in, pops, pops_sem)
    mask_copy = pltpu.make_async_copy(mask_in, mask, mask_sem)
    pops_copy.start()
    mask_copy.start()
    mask_copy.wait()
    core = lax.axis_index("core")
    for x in range(NX):
        rows = slice(2 * x, 2 * x + 2)
        to_low_y[19, rows, :] = mask[x, 0:2, :].astype(jnp.float32)
        to_high_y[19, rows, :] = mask[x, NY - 2 : NY, :].astype(jnp.float32)

    to_mate[...] = mask[(1 - core) * (NX - 1)].astype(jnp.float32)
    to_far[...] = mask[core * (NX - 1)].astype(jnp.float32)
    pops_copy.wait()
    for x in range(NX):
        rows = slice(2 * x, 2 * x + 2)
        for number in range(19):
            to_low_y[number, rows, :] = pops[number, x, 0:2, :]
            to_high_y[number, rows, :] = pops[number, x, NY - 2 : NY, :]


def pack_layers(pops, mask, low_y, high_y, out, up):
    pieces = ((low_y, 0, 2), (None, 2, 8), (None, 10, 8), (high_y, 2 + NY, 2))

    def piece(part, number, x, half):
        beside, start, size = part
        lanes = HALVES[half]
        if beside is not None:
            return beside[number, 2 * x : 2 * x + 2, lanes]
        if number < 19:
            return pops[number, x, start - 2 : start - 2 + size, lanes]
        return mask[x, start - 2 : start - 2 + size, lanes].astype(jnp.float32)

    def put(plane, part, half, value):
        row = (plane % 2) * ROWS + part[1]
        out[plane // 2, half, row : row + part[2], :] = value

    border, behind = (NX - 1, NX - 2) if up else (0, 1)
    for half in range(2):
        for part in pieces:
            for number in range(20):
                put(number, part, half, piece(part, number, border, half))
            f = [piece(part, number, behind, half) for number in range(19)]
            for i, number in enumerate(TOWARD_HIGH if up else TOWARD_LOW):
                put(20 + i, part, half, f[number])
            for i, value in enumerate(moments(f)[:4]):
                put(25 + i, part, half, value)
            put(29, part, half, piece(part, 19, behind, half))


def layers_kernel(pops, mask, low_y, high_y, sums, to_far, to_mate):
    core = lax.axis_index("core")
    for which in range(2):

        @pl.when(core == which)
        def _():
            pack_layers(pops, mask, low_y, high_y, to_mate, which == 0)
            pack_layers(pops, mask, low_y, high_y, to_far, which == 1)


def sums_kernel(pops, mask, low_y, high_y, far_mask, mate_mask, sums, flags):
    halves = HALVES
    core = lax.axis_index("core")
    first_core = core == 0
    low_x = jnp.where(first_core, far_mask[...], mate_mask[...])
    high_x = jnp.where(first_core, mate_mask[...], far_mask[...])
    flags[...] = jnp.zeros_like(flags)
    for half, lanes in enumerate(halves):
        for x in range(NX):
            row = FRONT + (x + 1) * ROWS
            flags[half, row + 1 : row + 2, :] = low_y[19, 2 * x + 1 : 2 * x + 2, lanes]
            flags[half, row + 2 : row + 2 + NY, :] = mask[x, :, lanes].astype(jnp.float32)
            flags[half, row + 2 + NY : row + 3 + NY, :] = high_y[19, 2 * x : 2 * x + 1, lanes]
        flags[half, FRONT + 2 : FRONT + 2 + NY, :] = low_x[:, lanes]
        row = FRONT + (NX + 1) * ROWS
        flags[half, row + 2 : row + 2 + NY, :] = high_x[:, lanes]
    lane = lax.broadcasted_iota(jnp.int32, (8, LANES), 1)
    numbers = [k for k in range(19) if VELOCITIES[k][1] != 0]
    acc = [jnp.zeros((8, LANES), jnp.float32) for _ in range(5)]
    for x in range(NX):
        for tile in range(NY // 8):
            row = FRONT + (x + 1) * ROWS + 2 + 8 * tile
            for half, lanes in enumerate(halves):
                f = [pops[k, x, 8 * tile : 8 * tile + 8, lanes] for k in range(19)]
                fluid = flags[half, row : row + 8, :]
                density, flux_y, coefs = response(numbers, f, fluid)
                acc[0] = acc[0] + fluid * flux_y
                acc[1] = acc[1] + fluid * density
                for number in numbers:
                    move_x, move_y, move_z = VELOCITIES[number]
                    start = row + move_x * ROWS + move_y
                    if move_z == 0:
                        ahead = flags[half, start : start + 8, :]
                    elif move_z == 1:
                        here = pltpu.roll(flags[half, start : start + 8, :], LANES - 1, 1)
                        if half == 0:
                            other = pltpu.roll(flags[1, start : start + 8, :], LANES - 1, 1)
                            ahead = jnp.where(lane == LANES - 1, other, here)
                        else:
                            ahead = jnp.where(lane == LANES - 1, 0.0, here)
                    else:
                        here = pltpu.roll(flags[half, start : start + 8, :], 1, 1)
                        if half == 1:
                            other = pltpu.roll(flags[0, start : start + 8, :], 1, 1)
                            ahead = jnp.where(lane == 0, other, here)
                        else:
                            ahead = jnp.where(lane == 0, 0.0, here)
                    sign = (2.0 * move_y) * ahead - move_y
                    for i in range(3):
                        acc[2 + i] = acc[2 + i] + sign * coefs[number][i]
    place = lax.broadcasted_iota(jnp.int32, (8, LANES), 0)
    for beside, y, sign, links in (
        (low_y, 0, 2.0, ((10, 1, low_x), (7, 2 * NX - 1, high_x))),
        (high_y, NY - 1, -2.0, ((8, 0, low_x), (9, 2 * NX - 2, high_x))),
    ):
        for lanes in halves:
            f = [beside[k, :, lanes] for k in range(19)]
            _, _, coefs = response([link[0] for link in links], f, beside[19, :, lanes])
            for number, row, layer in links:
                ahead = jnp.where(place == row, sign * layer[y : y + 1, lanes], 0.0)
                for i in range(3):
                    acc[2 + i] = acc[2 + i] + ahead * coefs[number][i]
    lane = lax.broadcasted_iota(jnp.int32, (1, LANES), 1)
    line = jnp.zeros((1, LANES), jnp.float32)
    for i in range(5):
        value = jnp.sum(acc[i], axis=0, keepdims=True)
        value = jnp.sum(value, axis=1, keepdims=True)
        line = jnp.where(lane == i, value, line)
    sums[...] = jnp.broadcast_to(line[None], sums.shape)


def relay_kernel(arrived, sums):
    sums[...] = jnp.broadcast_to(jnp.sum(arrived[...], axis=0, keepdims=True), sums.shape)


def gather_row(post, number, half, row):
    return post[number, half, row : row + 8, :]


def streamed(post, row, lane):
    result = [[None] * 19, [None] * 19]
    for number in range(19):
        move_x, move_y, move_z = VELOCITIES[number]
        start = row - move_x * ROWS - move_y
        if number == 0:
            for half in range(2):
                result[half][0] = gather_row(post, 0, half, row)
            continue
        first = gather_row(post, number, 0, start)
        second = gather_row(post, number, 1, start)
        if move_z == 1:
            first = pltpu.roll(first, 1, 1)
            second = pltpu.roll(second, 1, 1)
            second = jnp.where(lane == 0, first, second)
            first = jnp.where(lane == 0, SOLID, first)
        elif move_z == -1:
            first = pltpu.roll(first, LANES - 1, 1)
            second = pltpu.roll(second, LANES - 1, 1)
            first = jnp.where(lane == LANES - 1, second, first)
            second = jnp.where(lane == LANES - 1, SOLID, second)
        for half, value in enumerate((first, second)):
            own = gather_row(post, opposite_of(number), half, row)
            result[half][number] = jnp.where(value < LIMIT, value, own)
    return result


def outer_layer(beside, at, side, half, shift, post):
    core_rows = ((0, 8), (8, 8), (16, 4))
    for start, size in core_rows:

        def plane(number):
            row = (number % 2) * ROWS + start
            return beside[number // 2, half, row : row + size, :]

        density, flux_x, flux_y, flux_z = [plane(25 + i) for i in range(4)]
        fluid = plane(29)
        toward = 1.0 - 2.0 * side.astype(jnp.float32)
        inverse = 1.5 / (density + (1.0 - fluid))
        ux = flux_x * inverse * toward
        uy = flux_y * inverse + 1.5 * shift[:size]
        uz = flux_z * inverse
        base = 1.0 - (ux * ux + uy * uy + uz * uz) * (2.0 / 3.0)
        scaled = density * (1.0 / RELAX)
        for i, speed in enumerate((ux, ux + uy, ux - uy, ux + uz, ux - uz)):
            weight = scaled * (1.0 / 18.0 if i == 0 else 1.0 / 36.0)
            value = weight * (base + speed * (2.0 + 2.0 * speed)) - KEEP * plane(20 + i)
            number = TOWARD_HIGH[i] + side * (TOWARD_LOW[i] - TOWARD_HIGH[i])
            post[number, half, pl.ds(at + start, size), :] = jnp.where(fluid > 0.5, value, SOLID)


def steps_kernel(
    arrived, pops, mask, low_y, high_y, far, mate, out, post, later, flags, block, sems
):
    halves = HALVES
    sums = jnp.sum(arrived[...], axis=0)

    def total(i):
        return jnp.broadcast_to(sums[:, i : i + 1], (8, LANES))

    mass = total(1)
    drive = GAIN_RATE * (TARGET_SPEED - total(0) / mass)
    shift_1 = RELAX * drive
    momentum = total(2) + shift_1 * (total(3) + shift_1 * total(4))
    drive = GAIN_RATE * (TARGET_SPEED - momentum / mass)
    shift_2 = RELAX * drive
    lane = lax.broadcasted_iota(jnp.int32, (8, LANES), 1)

    for x in range(NX):
        for tile in range(NY // 8):
            row = FRONT + (x + 2) * ROWS + 2 + 8 * tile
            for half, lanes in enumerate(halves):
                f = [pops[k, x, 8 * tile : 8 * tile + 8, lanes] for k in range(19)]
                fluid = mask[x, 8 * tile : 8 * tile + 8, lanes].astype(jnp.float32)
                flags[half, row : row + 8, :] = fluid
                for number, value in enumerate(collide(f, fluid, shift_1)):
                    post[number, half, row : row + 8, :] = value
    for beside, start in ((low_y, 0), (high_y, 2 + NY)):
        for half, lanes in enumerate(halves):
            f = [beside[k, :, lanes] for k in range(19)]
            fluid = beside[19, :, lanes]
            value = collide(f, fluid, shift_1)
            for x in range(NX):
                row = FRONT + (x + 2) * ROWS + start
                flags[half, row : row + 2, :] = fluid[2 * x : 2 * x + 2]
                for number in range(19):
                    post[number, half, row : row + 2, :] = value[number][2 * x : 2 * x + 2]
    core = lax.axis_index("core")
    for beside, side in ((mate, 1 - core), (far, core)):
        inner = FRONT + ROWS + side * ((NX + 1) * ROWS)
        outer = FRONT + side * ((NX + 3) * ROWS)
        for half in range(2):
            for start, size in ((0, 8), (8, 8), (16, 4)):
                rows = pl.ds(inner + start, size)

                def plane(number):
                    row = (number % 2) * ROWS + start
                    return beside[number // 2, half, row : row + size, :]

                f = [plane(number) for number in range(19)]
                fluid = plane(19)
                flags[half, rows, :] = fluid
                for number, value in enumerate(collide(f, fluid, shift_1[:size])):
                    post[number, half, rows, :] = value
            outer_layer(beside, outer, side, half, shift_1, post)
    for tile in range((NX + 2) * ROWS // 8):
        row = FRONT + ROWS + 8 * tile
        f = streamed(post, row, lane)
        for half in range(2):
            fluid = flags[half, row : row + 8, :]
            for number, value in enumerate(collide(f[half], fluid, shift_2)):
                later[number, half, row : row + 8, :] = value
    for x in range(NX):
        for tile in range(NY // 8):
            row = FRONT + (x + 2) * ROWS + 2 + 8 * tile
            f = streamed(later, row, lane)
            for half, lanes in enumerate(halves):
                open_site = flags[half, row : row + 8, :] > 0.5
                for number in range(19):
                    block[x, number, 8 * tile : 8 * tile + 8, lanes] = jnp.where(
                        open_site, f[half][number], 0.0
                    )
        pltpu.make_async_copy(block.at[x], out.at[:, x], sems.at[x]).start()
    for x in range(NX):
        pltpu.make_async_copy(block.at[x], out.at[:, x], sems.at[x]).wait()


def f32(*shape):
    return jax.ShapeDtypeStruct(shape, jnp.float32)


def params():
    return pltpu.CompilerParams(vmem_limit_bytes=32 * 1024 * 1024)


def solution(mesh):
    regions, blocks = mesh.devices.shape
    cores = 2
    ring = 8 if blocks % 16 == 0 else 1
    grid = Mesh(
        mesh.devices.reshape(regions, blocks // (cores * ring), ring, cores),
        ("region", "x", "y", "core"),
    )
    local = ("x", "y", "core")
    first, second = blocks // cores, regions * cores

    def shifted(value, step):
        pairs = [(i, i + step) for i in range(regions) if 0 <= i + step < regions]
        return lax.ppermute(value, "region", pairs)

    def swapped(value, pairs):
        return lax.ppermute(value, local, pairs + [(j, i) for i, j in pairs])

    def from_mate(value):
        return swapped(value, [(i, i + 1) for i in range(0, blocks - 1, 2)])

    def from_far(value):
        return swapped(value, [(i, i + 1) for i in range(1, blocks - 1, 2)])

    def on_device(pops, mask):
        hbm = pl.BlockSpec(memory_space=pltpu.HBM)
        pops, mask, to_low_y, to_high_y, to_far, to_mate = pl.pallas_call(
            pack_kernel,
            out_shape=(
                f32(19, NX, NY, 2 * LANES),
                jax.ShapeDtypeStruct((NX, NY, 2 * LANES), jnp.int32),
                f32(20, 8, 256),
                f32(20, 8, 256),
                f32(NY, 2 * LANES),
                f32(NY, 2 * LANES),
            ),
            in_specs=[hbm, hbm],
            scratch_shapes=[pltpu.SemaphoreType.DMA, pltpu.SemaphoreType.DMA],
            compiler_params=params(),
        )(
            pltpu.with_memory_space_constraint(pops, pltpu.HBM),
            pltpu.with_memory_space_constraint(mask, pltpu.HBM),
        )
        low_y = shifted(to_high_y, 1)
        high_y = shifted(to_low_y, -1)
        far_mask = from_far(to_far)
        mate_mask = from_mate(to_mate)
        sums = pl.pallas_call(
            sums_kernel,
            out_shape=f32(first, 1, LANES),
            scratch_shapes=[pltpu.VMEM((2, FRONT + (NX + 2) * ROWS + 8, LANES), jnp.float32)],
            compiler_params=params(),
        )(pops, mask, low_y, high_y, far_mask, mate_mask)
        to_far, to_mate = pl.pallas_call(
            layers_kernel,
            out_shape=(f32(SLOTS, 2, 2 * ROWS, LANES), f32(SLOTS, 2, 2 * ROWS, LANES)),
            in_specs=[pl.BlockSpec(memory_space=pltpu.VMEM)] * 4 + [pl.BlockSpec(memory_space=pl.ANY)],
            compiler_params=params(),
        )(pops, mask, low_y, high_y, sums)
        far = from_far(to_far)
        mate = from_mate(to_mate)
        sums = lax.all_to_all(sums, ("x", "y"), 0, 0, tiled=True)
        sums = pl.pallas_call(
            relay_kernel, out_shape=f32(second, 1, LANES), compiler_params=params()
        )(sums)
        sums = lax.all_to_all(sums, ("region", "core"), 0, 0, tiled=True)
        rows = FRONT + (NX + 4) * ROWS + 8
        return pl.pallas_call(
            steps_kernel,
            out_shape=pltpu.HBM((19, NX, NY, 2 * LANES), jnp.float32),
            out_specs=hbm,
            scratch_shapes=[
                pltpu.VMEM((19, 2, rows, LANES), jnp.float32),
                pltpu.VMEM((19, 2, rows, LANES), jnp.float32),
                pltpu.VMEM((2, rows, LANES), jnp.float32),
                pltpu.VMEM((NX, 19, NY, 2 * LANES), jnp.float32),
                pltpu.SemaphoreType.DMA((NX,)),
            ],
            compiler_params=params(),
        )(sums, pops, mask, low_y, high_y, far, mate)

    return jax.shard_map(
        on_device,
        mesh=grid,
        in_specs=(P(None, local, "region", None), P(local, "region", None)),
        out_specs=P(None, local, "region", None),
        check_vma=False,
    )
```

```python
import jax
import jax.numpy as jnp
from jax import lax
from jax.experimental import pallas as pl
from jax.experimental.pallas import tpu as pltpu
from jax.sharding import Mesh
from jax.sharding import PartitionSpec as P

VELOCITIES = (
    (0, 0, 0),
    (1, 0, 0),
    (-1, 0, 0),
    (0, 1, 0),
    (0, -1, 0),
    (0, 0, 1),
    (0, 0, -1),
    (1, 1, 0),
    (-1, -1, 0),
    (1, -1, 0),
    (-1, 1, 0),
    (1, 0, 1),
    (-1, 0, -1),
    (1, 0, -1),
    (-1, 0, 1),
    (0, 1, 1),
    (0, -1, -1),
    (0, 1, -1),
    (0, -1, 1),
)
RELAX = 0.8
GAIN_RATE = 2.0
TARGET_SPEED = 0.05
KEEP = 1.0 / RELAX - 1.0

NX = 4
NY = 16
LANES = 128
ROWS = NY + 4
FRONT = 8
SOLID = 1e30
LIMIT = 1e29
HALVES = (slice(0, LANES), slice(LANES, 2 * LANES))
TOWARD_HIGH = (1, 7, 9, 11, 13)
TOWARD_LOW = (2, 10, 8, 14, 12)
SLOTS = 15


def opposite_of(number):
    if number == 0:
        return 0
    return number + 1 if number % 2 == 1 else number - 1


def moments(f):
    total = [None] + [f[k] + f[k + 1] for k in range(1, 19, 2)]
    diff = [None] + [f[k] - f[k + 1] for k in range(1, 19, 2)]
    density = f[0]
    for value in total[1:]:
        density = density + value
    flux_x = diff[1] + diff[4] + diff[5] + diff[6] + diff[7]
    flux_y = diff[2] + (diff[4] - diff[5]) + (diff[8] + diff[9])
    flux_z = diff[3] + (diff[6] - diff[7]) + (diff[8] - diff[9])
    return density, flux_x, flux_y, flux_z, total, diff


def collide(f, fluid, shift):
    density, flux_x, flux_y, flux_z, total, diff = moments(f)
    inverse = 1.0 / (density + (1.0 - fluid))
    inverse = inverse * 1.5
    ux = flux_x * inverse
    uy = flux_y * inverse + 1.5 * shift
    uz = flux_z * inverse
    square = ux * ux + uy * uy + uz * uz
    base = 1.0 - square * (2.0 / 3.0)
    scaled = density * (1.0 / RELAX)
    open_site = fluid > 0.5
    weight = (scaled * (1.0 / 3.0), scaled * (1.0 / 18.0), scaled * (1.0 / 36.0))
    base_1 = weight[1] * base
    base_2 = weight[2] * base
    twice_1 = weight[1] * 2.0
    twice_2 = weight[2] * 2.0
    post = [jnp.where(open_site, weight[0] * base - KEEP * f[0], SOLID)]
    along = (None, ux, uy, uz, ux + uy, ux - uy, ux + uz, ux - uz, uy + uz, uy - uz)
    for pair in range(1, 10):
        speed = along[pair]
        odd = speed * (twice_1 if pair <= 3 else twice_2)
        even = (base_1 if pair <= 3 else base_2) + odd * speed
        even = even - (0.5 * KEEP) * total[pair]
        odd = odd - (0.5 * KEEP) * diff[pair]
        post.append(jnp.where(open_site, even + odd, SOLID))
        post.append(jnp.where(open_site, even - odd, SOLID))
    return post


def response(numbers, f, fluid):
    density, flux_x, flux_y, flux_z, _, _ = moments(f)
    inverse = 1.0 / (density + (1.0 - fluid))
    ux = flux_x * inverse
    uy = flux_y * inverse
    uz = flux_z * inverse
    base = 1.0 - 1.5 * (ux * ux + uy * uy + uz * uz)
    scaled = density * (fluid * (1.0 / RELAX))
    result = {}
    for number in numbers:
        move_x, move_y, move_z = VELOCITIES[number]
        weight = scaled * (1.0 / 18.0 if number < 7 else 1.0 / 36.0)
        speed = move_y * uy
        if move_x:
            speed = speed + move_x * ux
        if move_z:
            speed = speed + move_z * uz
        zero = weight * (base + speed * (3.0 + 4.5 * speed)) - (KEEP * fluid) * f[number]
        one = weight * (3.0 * move_y + 9.0 * move_y * speed - 3.0 * uy)
        two = weight * 3.0
        result[number] = (zero, one, two)
    return density, flux_y, result


def pack_kernel(
    pops_in, mask_in, pops, mask, to_low_y, to_high_y, to_far, to_mate, pops_sem, mask_sem
):
    pops_copy = pltpu.make_async_copy(pops_in, pops, pops_sem)
    mask_copy = pltpu.make_async_copy(mask_in, mask, mask_sem)
    pops_copy.start()
    mask_copy.start()
    mask_copy.wait()
    core = lax.axis_index("core")
    for x in range(NX):
        rows = slice(2 * x, 2 * x + 2)
        to_low_y[19, rows, :] = mask[x, 0:2, :].astype(jnp.float32)
        to_high_y[19, rows, :] = mask[x, NY - 2 : NY, :].astype(jnp.float32)

    to_mate[...] = mask[(1 - core) * (NX - 1)].astype(jnp.float32)
    to_far[...] = mask[core * (NX - 1)].astype(jnp.float32)
    pops_copy.wait()
    for x in range(NX):
        rows = slice(2 * x, 2 * x + 2)
        for number in range(19):
            to_low_y[number, rows, :] = pops[number, x, 0:2, :]
            to_high_y[number, rows, :] = pops[number, x, NY - 2 : NY, :]


def pack_layers(pops, mask, low_y, high_y, out, up):
    pieces = ((low_y, 0, 2), (None, 2, 8), (None, 10, 8), (high_y, 2 + NY, 2))

    def piece(part, number, x, half):
        beside, start, size = part
        lanes = HALVES[half]
        if beside is not None:
            return beside[number, 2 * x : 2 * x + 2, lanes]
        if number < 19:
            return pops[number, x, start - 2 : start - 2 + size, lanes]
        return mask[x, start - 2 : start - 2 + size, lanes].astype(jnp.float32)

    def put(plane, part, half, value):
        row = (plane % 2) * ROWS + part[1]
        out[plane // 2, half, row : row + part[2], :] = value

    border, behind = (NX - 1, NX - 2) if up else (0, 1)
    for half in range(2):
        for part in pieces:
            for number in range(20):
                put(number, part, half, piece(part, number, border, half))
            f = [piece(part, number, behind, half) for number in range(19)]
            for i, number in enumerate(TOWARD_HIGH if up else TOWARD_LOW):
                put(20 + i, part, half, f[number])
            for i, value in enumerate(moments(f)[:4]):
                put(25 + i, part, half, value)
            put(29, part, half, piece(part, 19, behind, half))


def layers_kernel(pops, mask, low_y, high_y, sums, to_far, to_mate):
    core = lax.axis_index("core")
    for which in range(2):

        @pl.when(core == which)
        def _():
            pack_layers(pops, mask, low_y, high_y, to_mate, which == 0)
            pack_layers(pops, mask, low_y, high_y, to_far, which == 1)


def sums_kernel(pops, mask, low_y, high_y, far_mask, mate_mask, sums, flags):
    halves = HALVES
    core = lax.axis_index("core")
    first_core = core == 0
    low_x = jnp.where(first_core, far_mask[...], mate_mask[...])
    high_x = jnp.where(first_core, mate_mask[...], far_mask[...])
    flags[...] = jnp.zeros_like(flags)
    for half, lanes in enumerate(halves):
        for x in range(NX):
            row = FRONT + (x + 1) * ROWS
            flags[half, row + 1 : row + 2, :] = low_y[19, 2 * x + 1 : 2 * x + 2, lanes]
            flags[half, row + 2 : row + 2 + NY, :] = mask[x, :, lanes].astype(jnp.float32)
            flags[half, row + 2 + NY : row + 3 + NY, :] = high_y[19, 2 * x : 2 * x + 1, lanes]
        flags[half, FRONT + 2 : FRONT + 2 + NY, :] = low_x[:, lanes]
        row = FRONT + (NX + 1) * ROWS
        flags[half, row + 2 : row + 2 + NY, :] = high_x[:, lanes]
    lane = lax.broadcasted_iota(jnp.int32, (8, LANES), 1)
    numbers = [k for k in range(19) if VELOCITIES[k][1] != 0]
    acc = [jnp.zeros((8, LANES), jnp.float32) for _ in range(5)]
    for x in range(NX):
        for tile in range(NY // 8):
            row = FRONT + (x + 1) * ROWS + 2 + 8 * tile
            for half, lanes in enumerate(halves):
                f = [pops[k, x, 8 * tile : 8 * tile + 8, lanes] for k in range(19)]
                fluid = flags[half, row : row + 8, :]
                density, flux_y, coefs = response(numbers, f, fluid)
                acc[0] = acc[0] + fluid * flux_y
                acc[1] = acc[1] + fluid * density
                for number in numbers:
                    move_x, move_y, move_z = VELOCITIES[number]
                    start = row + move_x * ROWS + move_y
                    if move_z == 0:
                        ahead = flags[half, start : start + 8, :]
                    elif move_z == 1:
                        here = pltpu.roll(flags[half, start : start + 8, :], LANES - 1, 1)
                        if half == 0:
                            other = pltpu.roll(flags[1, start : start + 8, :], LANES - 1, 1)
                            ahead = jnp.where(lane == LANES - 1, other, here)
                        else:
                            ahead = jnp.where(lane == LANES - 1, 0.0, here)
                    else:
                        here = pltpu.roll(flags[half, start : start + 8, :], 1, 1)
                        if half == 1:
                            other = pltpu.roll(flags[0, start : start + 8, :], 1, 1)
                            ahead = jnp.where(lane == 0, other, here)
                        else:
                            ahead = jnp.where(lane == 0, 0.0, here)
                    sign = (2.0 * move_y) * ahead - move_y
                    for i in range(3):
                        acc[2 + i] = acc[2 + i] + sign * coefs[number][i]
    place = lax.broadcasted_iota(jnp.int32, (8, LANES), 0)
    for beside, y, sign, links in (
        (low_y, 0, 2.0, ((10, 1, low_x), (7, 2 * NX - 1, high_x))),
        (high_y, NY - 1, -2.0, ((8, 0, low_x), (9, 2 * NX - 2, high_x))),
    ):
        for lanes in halves:
            f = [beside[k, :, lanes] for k in range(19)]
            _, _, coefs = response([link[0] for link in links], f, beside[19, :, lanes])
            for number, row, layer in links:
                ahead = jnp.where(place == row, sign * layer[y : y + 1, lanes], 0.0)
                for i in range(3):
                    acc[2 + i] = acc[2 + i] + ahead * coefs[number][i]
    lane = lax.broadcasted_iota(jnp.int32, (1, LANES), 1)
    line = jnp.zeros((1, LANES), jnp.float32)
    for i in range(5):
        value = jnp.sum(acc[i], axis=0, keepdims=True)
        value = jnp.sum(value, axis=1, keepdims=True)
        line = jnp.where(lane == i, value, line)
    sums[...] = jnp.broadcast_to(line[None], sums.shape)


def relay_kernel(arrived, sums):
    sums[...] = jnp.broadcast_to(jnp.sum(arrived[...], axis=0, keepdims=True), sums.shape)


def gather_row(post, number, half, row):
    return post[number, half, row : row + 8, :]


def streamed(post, row, lane):
    result = [[None] * 19, [None] * 19]
    for number in range(19):
        move_x, move_y, move_z = VELOCITIES[number]
        start = row - move_x * ROWS - move_y
        if number == 0:
            for half in range(2):
                result[half][0] = gather_row(post, 0, half, row)
            continue
        first = gather_row(post, number, 0, start)
        second = gather_row(post, number, 1, start)
        if move_z == 1:
            first = pltpu.roll(first, 1, 1)
            second = pltpu.roll(second, 1, 1)
            second = jnp.where(lane == 0, first, second)
            first = jnp.where(lane == 0, SOLID, first)
        elif move_z == -1:
            first = pltpu.roll(first, LANES - 1, 1)
            second = pltpu.roll(second, LANES - 1, 1)
            first = jnp.where(lane == LANES - 1, second, first)
            second = jnp.where(lane == LANES - 1, SOLID, second)
        for half, value in enumerate((first, second)):
            own = gather_row(post, opposite_of(number), half, row)
            result[half][number] = jnp.where(value < LIMIT, value, own)
    return result


def outer_layer(beside, at, side, half, shift, post):
    core_rows = ((0, 8), (8, 8), (16, 4))
    for start, size in core_rows:

        def plane(number):
            row = (number % 2) * ROWS + start
            return beside[number // 2, half, row : row + size, :]

        density, flux_x, flux_y, flux_z = [plane(25 + i) for i in range(4)]
        fluid = plane(29)
        toward = 1.0 - 2.0 * side.astype(jnp.float32)
        inverse = 1.5 / (density + (1.0 - fluid))
        ux = flux_x * inverse * toward
        uy = flux_y * inverse + 1.5 * shift[:size]
        uz = flux_z * inverse
        base = 1.0 - (ux * ux + uy * uy + uz * uz) * (2.0 / 3.0)
        scaled = density * (1.0 / RELAX)
        for i, speed in enumerate((ux, ux + uy, ux - uy, ux + uz, ux - uz)):
            weight = scaled * (1.0 / 18.0 if i == 0 else 1.0 / 36.0)
            value = weight * (base + speed * (2.0 + 2.0 * speed)) - KEEP * plane(20 + i)
            number = TOWARD_HIGH[i] + side * (TOWARD_LOW[i] - TOWARD_HIGH[i])
            post[number, half, pl.ds(at + start, size), :] = jnp.where(fluid > 0.5, value, SOLID)


def last_streaming(later, flags, block, x, lane):
    for tile in range(NY // 8):
        row = FRONT + (x + 2) * ROWS + 2 + 8 * tile
        f = streamed(later, row, lane)
        for half, lanes in enumerate(HALVES):
            open_site = flags[half, row : row + 8, :] > 0.5
            for number in range(19):
                block[x, number, 8 * tile : 8 * tile + 8, lanes] = jnp.where(
                    open_site, f[half][number], 0.0
                )


def steps_kernel(
    arrived, pops, mask, low_y, high_y, far, mate, out, post, later, flags, block, sems
):
    halves = HALVES
    sums = jnp.sum(arrived[...], axis=0)

    def total(i):
        return jnp.broadcast_to(sums[:, i : i + 1], (8, LANES))

    mass = total(1)
    drive = GAIN_RATE * (TARGET_SPEED - total(0) / mass)
    shift_1 = RELAX * drive
    momentum = total(2) + shift_1 * (total(3) + shift_1 * total(4))
    drive = GAIN_RATE * (TARGET_SPEED - momentum / mass)
    shift_2 = RELAX * drive
    lane = lax.broadcasted_iota(jnp.int32, (8, LANES), 1)

    for x in range(NX):
        for tile in range(NY // 8):
            row = FRONT + (x + 2) * ROWS + 2 + 8 * tile
            for half, lanes in enumerate(halves):
                f = [pops[k, x, 8 * tile : 8 * tile + 8, lanes] for k in range(19)]
                fluid = mask[x, 8 * tile : 8 * tile + 8, lanes].astype(jnp.float32)
                flags[half, row : row + 8, :] = fluid
                for number, value in enumerate(collide(f, fluid, shift_1)):
                    post[number, half, row : row + 8, :] = value
    for beside, start in ((low_y, 0), (high_y, 2 + NY)):
        for half, lanes in enumerate(halves):
            f = [beside[k, :, lanes] for k in range(19)]
            fluid = beside[19, :, lanes]
            value = collide(f, fluid, shift_1)
            for x in range(NX):
                row = FRONT + (x + 2) * ROWS + start
                flags[half, row : row + 2, :] = fluid[2 * x : 2 * x + 2]
                for number in range(19):
                    post[number, half, row : row + 2, :] = value[number][2 * x : 2 * x + 2]
    core = lax.axis_index("core")
    for beside, side in ((mate, 1 - core), (far, core)):
        inner = FRONT + ROWS + side * ((NX + 1) * ROWS)
        outer = FRONT + side * ((NX + 3) * ROWS)
        for half in range(2):
            for start, size in ((0, 8), (8, 8), (16, 4)):
                rows = pl.ds(inner + start, size)

                def plane(number):
                    row = (number % 2) * ROWS + start
                    return beside[number // 2, half, row : row + size, :]

                f = [plane(number) for number in range(19)]
                fluid = plane(19)
                flags[half, rows, :] = fluid
                for number, value in enumerate(collide(f, fluid, shift_1[:size])):
                    post[number, half, rows, :] = value
            outer_layer(beside, outer, side, half, shift_1, post)
    done = 0
    for tile in range((NX + 2) * ROWS // 8):
        row = FRONT + ROWS + 8 * tile
        f = streamed(post, row, lane)
        for half in range(2):
            fluid = flags[half, row : row + 8, :]
            for number, value in enumerate(collide(f[half], fluid, shift_2)):
                later[number, half, row : row + 8, :] = value
        while done < NX and row + 8 >= FRONT + (done + 4) * ROWS:
            last_streaming(later, flags, block, done, lane)
            pltpu.make_async_copy(block.at[done], out.at[:, done], sems.at[done]).start()
            done += 1
    for x in range(NX):
        pltpu.make_async_copy(block.at[x], out.at[:, x], sems.at[x]).wait()


def f32(*shape):
    return jax.ShapeDtypeStruct(shape, jnp.float32)


def params():
    return pltpu.CompilerParams(vmem_limit_bytes=32 * 1024 * 1024)


def solution(mesh):
    regions, blocks = mesh.devices.shape
    cores = 2
    ring = 8 if blocks % 16 == 0 else 1
    grid = Mesh(
        mesh.devices.reshape(regions, blocks // (cores * ring), ring, cores),
        ("region", "x", "y", "core"),
    )
    local = ("x", "y", "core")
    first, second = blocks // cores, regions * cores

    def shifted(value, step):
        pairs = [(i, i + step) for i in range(regions) if 0 <= i + step < regions]
        return lax.ppermute(value, "region", pairs)

    def swapped(value, pairs):
        return lax.ppermute(value, local, pairs + [(j, i) for i, j in pairs])

    def from_mate(value):
        return swapped(value, [(i, i + 1) for i in range(0, blocks - 1, 2)])

    def from_far(value):
        return swapped(value, [(i, i + 1) for i in range(1, blocks - 1, 2)])

    def on_device(pops, mask):
        hbm = pl.BlockSpec(memory_space=pltpu.HBM)
        pops, mask, to_low_y, to_high_y, to_far, to_mate = pl.pallas_call(
            pack_kernel,
            out_shape=(
                f32(19, NX, NY, 2 * LANES),
                jax.ShapeDtypeStruct((NX, NY, 2 * LANES), jnp.int32),
                f32(20, 8, 256),
                f32(20, 8, 256),
                f32(NY, 2 * LANES),
                f32(NY, 2 * LANES),
            ),
            in_specs=[hbm, hbm],
            scratch_shapes=[pltpu.SemaphoreType.DMA, pltpu.SemaphoreType.DMA],
            compiler_params=params(),
        )(
            pltpu.with_memory_space_constraint(pops, pltpu.HBM),
            pltpu.with_memory_space_constraint(mask, pltpu.HBM),
        )
        low_y = shifted(to_high_y, 1)
        high_y = shifted(to_low_y, -1)
        far_mask = from_far(to_far)
        mate_mask = from_mate(to_mate)
        sums = pl.pallas_call(
            sums_kernel,
            out_shape=f32(first, 1, LANES),
            scratch_shapes=[pltpu.VMEM((2, FRONT + (NX + 2) * ROWS + 8, LANES), jnp.float32)],
            compiler_params=params(),
        )(pops, mask, low_y, high_y, far_mask, mate_mask)
        to_far, to_mate = pl.pallas_call(
            layers_kernel,
            out_shape=(f32(SLOTS, 2, 2 * ROWS, LANES), f32(SLOTS, 2, 2 * ROWS, LANES)),
            in_specs=[pl.BlockSpec(memory_space=pltpu.VMEM)] * 4 + [pl.BlockSpec(memory_space=pl.ANY)],
            compiler_params=params(),
        )(pops, mask, low_y, high_y, sums)
        far = from_far(to_far)
        mate = from_mate(to_mate)
        sums = lax.all_to_all(sums, ("x", "y"), 0, 0, tiled=True)
        sums = pl.pallas_call(
            relay_kernel,
            out_shape=f32(second, 1, LANES),
            compiler_params=params(),
            cost_estimate=pl.CostEstimate(flops=3 * 10**10, bytes_accessed=0, transcendentals=0),
        )(sums)
        sums = lax.all_to_all(sums, ("region", "core"), 0, 0, tiled=True)
        rows = FRONT + (NX + 4) * ROWS + 8
        return pl.pallas_call(
            steps_kernel,
            out_shape=pltpu.HBM((19, NX, NY, 2 * LANES), jnp.float32),
            out_specs=hbm,
            scratch_shapes=[
                pltpu.VMEM((19, 2, rows, LANES), jnp.float32),
                pltpu.VMEM((19, 2, rows, LANES), jnp.float32),
                pltpu.VMEM((2, rows, LANES), jnp.float32),
                pltpu.VMEM((NX, 19, NY, 2 * LANES), jnp.float32),
                pltpu.SemaphoreType.DMA((NX,)),
            ],
            compiler_params=params(),
        )(sums, pops, mask, low_y, high_y, far, mate)

    return jax.shard_map(
        on_device,
        mesh=grid,
        in_specs=(P(None, local, "region", None), P(local, "region", None)),
        out_specs=P(None, local, "region", None),
        check_vma=False,
    )
```

```python
import jax
import jax.numpy as jnp
from jax import lax
from jax.experimental import pallas as pl
from jax.experimental.pallas import tpu as pltpu
from jax.sharding import Mesh
from jax.sharding import PartitionSpec as P

VELOCITIES = (
    (0, 0, 0),
    (1, 0, 0),
    (-1, 0, 0),
    (0, 1, 0),
    (0, -1, 0),
    (0, 0, 1),
    (0, 0, -1),
    (1, 1, 0),
    (-1, -1, 0),
    (1, -1, 0),
    (-1, 1, 0),
    (1, 0, 1),
    (-1, 0, -1),
    (1, 0, -1),
    (-1, 0, 1),
    (0, 1, 1),
    (0, -1, -1),
    (0, 1, -1),
    (0, -1, 1),
)
RELAX = 0.8
GAIN_RATE = 2.0
TARGET_SPEED = 0.05
KEEP = 1.0 / RELAX - 1.0

NX = 4
NY = 16
LANES = 128
ROWS = NY + 4
FRONT = 8
SOLID = 1e30
LIMIT = 1e29
HALVES = (slice(0, LANES), slice(LANES, 2 * LANES))
TOWARD_HIGH = (1, 7, 9, 11, 13)
TOWARD_LOW = (2, 10, 8, 14, 12)
UPWARD = (3, 7, 10, 15, 17)
DOWNWARD = (4, 9, 8, 18, 16)
SPARE = (0, 1, 2, 5)
SLOTS = 15


def opposite_of(number):
    if number == 0:
        return 0
    return number + 1 if number % 2 == 1 else number - 1


def moments(f):
    total = [None] + [f[k] + f[k + 1] for k in range(1, 19, 2)]
    diff = [None] + [f[k] - f[k + 1] for k in range(1, 19, 2)]
    density = f[0]
    for value in total[1:]:
        density = density + value
    flux_x = diff[1] + diff[4] + diff[5] + diff[6] + diff[7]
    flux_y = diff[2] + (diff[4] - diff[5]) + (diff[8] + diff[9])
    flux_z = diff[3] + (diff[6] - diff[7]) + (diff[8] - diff[9])
    return density, flux_x, flux_y, flux_z, total, diff


def collide(f, fluid, shift):
    density, flux_x, flux_y, flux_z, total, diff = moments(f)
    inverse = 1.0 / (density + (1.0 - fluid))
    inverse = inverse * 1.5
    ux = flux_x * inverse
    uy = flux_y * inverse + 1.5 * shift
    uz = flux_z * inverse
    square = ux * ux + uy * uy + uz * uz
    base = 1.0 - square * (2.0 / 3.0)
    open_site = fluid > 0.5
    scaled = jnp.where(open_site, density * (1.0 / RELAX), 0.0)
    weight = (scaled * (1.0 / 3.0), scaled * (1.0 / 18.0), scaled * (1.0 / 36.0))
    base_0, base_1, base_2 = (jnp.where(open_site, w * base, SOLID) for w in weight)
    twice_1 = weight[1] * 2.0
    twice_2 = weight[2] * 2.0
    post = [base_0 - KEEP * f[0]]
    along = (None, ux, uy, uz, ux + uy, ux - uy, ux + uz, ux - uz, uy + uz, uy - uz)
    for pair in range(1, 10):
        speed = along[pair]
        odd = speed * (twice_1 if pair <= 3 else twice_2)
        even = (base_1 if pair <= 3 else base_2) + odd * speed
        even = even - (0.5 * KEEP) * total[pair]
        odd = odd - (0.5 * KEEP) * diff[pair]
        post.append(even + odd)
        post.append(even - odd)
    return post


def response(numbers, f, fluid):
    density, flux_x, flux_y, flux_z, _, _ = moments(f)
    inverse = 1.0 / (density + (1.0 - fluid))
    ux = flux_x * inverse
    uy = flux_y * inverse
    uz = flux_z * inverse
    base = 1.0 - 1.5 * (ux * ux + uy * uy + uz * uz)
    scaled = density * (fluid * (1.0 / RELAX))
    result = {}
    for number in numbers:
        move_x, move_y, move_z = VELOCITIES[number]
        weight = scaled * (1.0 / 18.0 if number < 7 else 1.0 / 36.0)
        speed = move_y * uy
        if move_x:
            speed = speed + move_x * ux
        if move_z:
            speed = speed + move_z * uz
        zero = weight * (base + speed * (3.0 + 4.5 * speed)) - (KEEP * fluid) * f[number]
        one = weight * (3.0 * move_y + 9.0 * move_y * speed - 3.0 * uy)
        two = weight * 3.0
        result[number] = (zero, one, two)
    return density, flux_y, result


def pack_kernel(
    pops_in, mask_in, pops, mask, to_low_y, to_high_y, to_far, to_mate, pops_sem, mask_sem
):
    pops_copy = pltpu.make_async_copy(pops_in, pops, pops_sem)
    mask_copy = pltpu.make_async_copy(mask_in, mask, mask_sem)
    pops_copy.start()
    mask_copy.start()
    mask_copy.wait()
    core = lax.axis_index("core")
    to_mate[...] = mask[(1 - core) * (NX - 1)].astype(jnp.float32)
    to_far[...] = mask[core * (NX - 1)].astype(jnp.float32)
    pops_copy.wait()
    for out, border, behind, numbers in (
        (to_low_y, 0, 1, DOWNWARD),
        (to_high_y, NY - 1, NY - 2, UPWARD),
    ):
        for x in range(NX):
            f = [pops[number, x, behind : behind + 1, :] for number in range(19)]
            planes = [pops[number, x, border : border + 1, :] for number in range(19)]
            planes.append(mask[x, border : border + 1, :].astype(jnp.float32))
            planes += [f[number] for number in numbers]
            planes += list(moments(f)[:4])
            planes.append(mask[x, behind : behind + 1, :].astype(jnp.float32))
            for i, value in enumerate(planes):
                row = NX * (i % 2) + x
                out[i // 2, row : row + 1, :] = value


def y_plane(beside, plane, lanes, x=None):
    first = NX * (plane % 2)
    if x is None:
        return beside[plane // 2, first : first + NX, lanes]
    return beside[plane // 2, first + x : first + x + 1, lanes]


def pack_layers(pops, mask, low_y, high_y, out, up):
    border, behind = (NX - 1, NX - 2) if up else (0, 1)
    toward = TOWARD_HIGH if up else TOWARD_LOW

    def put(plane, start, half, value):
        row = (plane % 2) * ROWS + start
        out[plane // 2, half, row : row + value.shape[0], :] = value

    for half, lanes in enumerate(HALVES):
        for tile in range(NY // 8):
            rows = slice(8 * tile, 8 * tile + 8)
            start = 2 + 8 * tile
            for number in range(19):
                put(number, start, half, pops[number, border, rows, lanes])
            put(19, start, half, mask[border, rows, lanes].astype(jnp.float32))
            f = [pops[number, behind, rows, lanes] for number in range(19)]
            for i, number in enumerate(toward):
                put(20 + i, start, half, f[number])
            for i, value in enumerate(moments(f)[:4]):
                put(25 + i, start, half, value)
            put(29, start, half, mask[behind, rows, lanes].astype(jnp.float32))
        for beside, inner, outer, numbers in (
            (low_y, 1, 0, UPWARD),
            (high_y, 2 + NY, 3 + NY, DOWNWARD),
        ):
            for number in range(20):
                put(number, inner, half, y_plane(beside, number, lanes, border))
            for i, number in enumerate(numbers):
                put(number, outer, half, y_plane(beside, 20 + i, lanes, border))
            for i, number in enumerate(SPARE):
                put(number, outer, half, y_plane(beside, 25 + i, lanes, border))
            put(19, outer, half, y_plane(beside, 29, lanes, border))
            f = [y_plane(beside, number, lanes, behind) for number in range(19)]
            for i, number in enumerate(toward):
                put(20 + i, inner, half, f[number])
                place = numbers.index(number) if number in numbers else 0
                put(20 + i, outer, half, y_plane(beside, 20 + place, lanes, behind))
            for i, value in enumerate(moments(f)[:4]):
                put(25 + i, inner, half, value)
                put(25 + i, outer, half, y_plane(beside, 25 + i, lanes, behind))
            put(29, inner, half, y_plane(beside, 19, lanes, behind))
            put(29, outer, half, y_plane(beside, 29, lanes, behind))


def layers_kernel(pops, mask, low_y, high_y, sums, to_far, to_mate):
    core = lax.axis_index("core")
    for which in range(2):

        @pl.when(core == which)
        def _():
            pack_layers(pops, mask, low_y, high_y, to_mate, which == 0)
            pack_layers(pops, mask, low_y, high_y, to_far, which == 1)


def sums_kernel(pops, mask, low_y, high_y, far_mask, chip_masks, sums, flags):
    halves = HALVES
    core = lax.axis_index("core")
    first_core = core == 0
    mate_mask = chip_masks[1 - core]
    low_x = jnp.where(first_core, far_mask[...], mate_mask)
    high_x = jnp.where(first_core, mate_mask, far_mask[...])
    flags[...] = jnp.zeros_like(flags)
    for half, lanes in enumerate(halves):
        for x in range(NX):
            row = FRONT + (x + 1) * ROWS
            flags[half, row + 1 : row + 2, :] = y_plane(low_y, 19, lanes, x)
            flags[half, row + 2 : row + 2 + NY, :] = mask[x, :, lanes].astype(jnp.float32)
            flags[half, row + 2 + NY : row + 3 + NY, :] = y_plane(high_y, 19, lanes, x)
        flags[half, FRONT + 2 : FRONT + 2 + NY, :] = low_x[:, lanes]
        row = FRONT + (NX + 1) * ROWS
        flags[half, row + 2 : row + 2 + NY, :] = high_x[:, lanes]
    lane = lax.broadcasted_iota(jnp.int32, (8, LANES), 1)
    numbers = [k for k in range(19) if VELOCITIES[k][1] != 0]
    acc = [jnp.zeros((8, LANES), jnp.float32) for _ in range(5)]
    for x in range(NX):
        for tile in range(NY // 8):
            row = FRONT + (x + 1) * ROWS + 2 + 8 * tile
            for half, lanes in enumerate(halves):
                f = [pops[k, x, 8 * tile : 8 * tile + 8, lanes] for k in range(19)]
                fluid = flags[half, row : row + 8, :]
                density, flux_y, coefs = response(numbers, f, fluid)
                acc[0] = acc[0] + fluid * flux_y
                acc[1] = acc[1] + fluid * density
                for number in numbers:
                    move_x, move_y, move_z = VELOCITIES[number]
                    start = row + move_x * ROWS + move_y
                    if move_z == 0:
                        ahead = flags[half, start : start + 8, :]
                    elif move_z == 1:
                        here = pltpu.roll(flags[half, start : start + 8, :], LANES - 1, 1)
                        if half == 0:
                            other = pltpu.roll(flags[1, start : start + 8, :], LANES - 1, 1)
                            ahead = jnp.where(lane == LANES - 1, other, here)
                        else:
                            ahead = jnp.where(lane == LANES - 1, 0.0, here)
                    else:
                        here = pltpu.roll(flags[half, start : start + 8, :], 1, 1)
                        if half == 1:
                            other = pltpu.roll(flags[0, start : start + 8, :], 1, 1)
                            ahead = jnp.where(lane == 0, other, here)
                        else:
                            ahead = jnp.where(lane == 0, 0.0, here)
                    sign = (2.0 * move_y) * ahead - move_y
                    for i in range(3):
                        acc[2 + i] = acc[2 + i] + sign * coefs[number][i]
    extra = [jnp.zeros((1, LANES), jnp.float32) for _ in range(3)]
    for beside, y, sign, links in (
        (low_y, 0, 2.0, ((10, 0, low_x), (7, NX - 1, high_x))),
        (high_y, NY - 1, -2.0, ((8, 0, low_x), (9, NX - 1, high_x))),
    ):
        for lanes in halves:
            for number, x, layer in links:
                f = [y_plane(beside, k, lanes, x) for k in range(19)]
                _, _, coefs = response((number,), f, y_plane(beside, 19, lanes, x))
                ahead = sign * layer[y : y + 1, lanes]
                for i in range(3):
                    extra[i] = extra[i] + ahead * coefs[number][i]
    lane = lax.broadcasted_iota(jnp.int32, (1, LANES), 1)
    line = jnp.zeros((1, LANES), jnp.float32)
    for i in range(5):
        value = jnp.sum(acc[i], axis=0, keepdims=True)
        if i >= 2:
            value = value + extra[i - 2]
        value = jnp.sum(value, axis=1, keepdims=True)
        line = jnp.where(lane == i, value, line)
    sums[...] = jnp.broadcast_to(line[None], sums.shape)


def relay_kernel(arrived, sums):
    sums[...] = jnp.broadcast_to(jnp.sum(arrived[...], axis=0, keepdims=True), sums.shape)


def gather_row(post, number, half, row):
    return post[number, half, row : row + 8, :]


def streamed(post, row, lane):
    result = [[None] * 19, [None] * 19]
    for number in range(19):
        move_x, move_y, move_z = VELOCITIES[number]
        start = row - move_x * ROWS - move_y
        if number == 0:
            for half in range(2):
                result[half][0] = gather_row(post, 0, half, row)
            continue
        first = gather_row(post, number, 0, start)
        second = gather_row(post, number, 1, start)
        if move_z == 1:
            first = pltpu.roll(first, 1, 1)
            second = pltpu.roll(second, 1, 1)
            second = jnp.where(lane == 0, first, second)
            first = jnp.where(lane == 0, SOLID, first)
        elif move_z == -1:
            first = pltpu.roll(first, LANES - 1, 1)
            second = pltpu.roll(second, LANES - 1, 1)
            first = jnp.where(lane == LANES - 1, second, first)
            second = jnp.where(lane == LANES - 1, SOLID, second)
        for half, value in enumerate((first, second)):
            own = gather_row(post, opposite_of(number), half, row)
            result[half][number] = jnp.where(value < LIMIT, value, own)
    return result


def arriving(f, fluid, flow, speeds, shift):
    density, flux_x, flux_y, flux_z = flow
    inverse = 1.5 / (density + (1.0 - fluid))
    ux = flux_x * inverse
    uy = flux_y * inverse + 1.5 * shift
    uz = flux_z * inverse
    base = 1.0 - (ux * ux + uy * uy + uz * uz) * (2.0 / 3.0)
    scaled = density * (1.0 / RELAX)
    result = []
    for i, speed in enumerate(speeds(ux, uy, uz)):
        weight = scaled * (1.0 / 18.0 if i == 0 else 1.0 / 36.0)
        value = weight * (base + speed * (2.0 + 2.0 * speed)) - KEEP * f[i]
        result.append(jnp.where(fluid > 0.5, value, SOLID))
    return result


def along_x(sign):
    return lambda ux, uy, uz: (
        sign * ux,
        sign * ux + uy,
        sign * ux - uy,
        sign * ux + uz,
        sign * ux - uz,
    )


def along_y(sign):
    return lambda ux, uy, uz: (
        sign * uy,
        sign * uy + ux,
        sign * uy - ux,
        sign * uy + uz,
        sign * uy - uz,
    )


def x_plane(beside, plane, half, start, size):
    row = (plane % 2) * ROWS + start
    return beside[plane // 2, half, row : row + size, :]


def last_streaming(later, flags, block, x, lane):
    for tile in range(NY // 8):
        row = FRONT + (x + 2) * ROWS + 2 + 8 * tile
        f = streamed(later, row, lane)
        for half, lanes in enumerate(HALVES):
            open_site = flags[half, row : row + 8, :] > 0.5
            for number in range(19):
                block[x, number, 8 * tile : 8 * tile + 8, lanes] = jnp.where(
                    open_site, f[half][number], 0.0
                )


def steps_kernel(
    arrived, pops, mask, low_y, high_y, far, mate, out, post, later, flags, block, sems
):
    halves = HALVES
    sums = jnp.sum(arrived[...], axis=0)

    def total(i):
        return jnp.broadcast_to(sums[:, i : i + 1], (8, LANES))

    mass = total(1)
    drive = GAIN_RATE * (TARGET_SPEED - total(0) / mass)
    shift_1 = RELAX * drive
    momentum = total(2) + shift_1 * (total(3) + shift_1 * total(4))
    drive = GAIN_RATE * (TARGET_SPEED - momentum / mass)
    shift_2 = RELAX * drive
    lane = lax.broadcasted_iota(jnp.int32, (8, LANES), 1)

    for x in range(NX):
        for tile in range(NY // 8):
            row = FRONT + (x + 2) * ROWS + 2 + 8 * tile
            for half, lanes in enumerate(halves):
                f = [pops[k, x, 8 * tile : 8 * tile + 8, lanes] for k in range(19)]
                fluid = mask[x, 8 * tile : 8 * tile + 8, lanes].astype(jnp.float32)
                flags[half, row : row + 8, :] = fluid
                for number, value in enumerate(collide(f, fluid, shift_1)):
                    post[number, half, row : row + 8, :] = value
    first_row = FRONT + 2 * ROWS
    for beside, inner, outer, numbers, sign in (
        (low_y, 1, 0, UPWARD, 1.0),
        (high_y, 2 + NY, 3 + NY, DOWNWARD, -1.0),
    ):
        for half, lanes in enumerate(halves):
            planes = [y_plane(beside, i, lanes) for i in range(30)]
            value = collide(planes[:19], planes[19], shift_1[:NX])
            moved = arriving(
                planes[20:25], planes[29], planes[25:29], along_y(sign), shift_1[:NX]
            )
            for x in range(NX):
                row = first_row + x * ROWS + inner
                flags[half, row : row + 1, :] = planes[19][x : x + 1]
                for number in range(19):
                    post[number, half, row : row + 1, :] = value[number][x : x + 1]
                row = first_row + x * ROWS + outer
                flags[half, row : row + 1, :] = planes[29][x : x + 1]
                for i, number in enumerate(numbers):
                    post[number, half, row : row + 1, :] = moved[i][x : x + 1]
    core = lax.axis_index("core")
    for beside, side in ((mate, 1 - core), (far, core)):
        inner = FRONT + ROWS + side * ((NX + 1) * ROWS)
        outer = FRONT + side * ((NX + 3) * ROWS)
        sign = 1.0 - 2.0 * side.astype(jnp.float32)
        for half in range(2):
            for start, size in ((1, 8), (9, 8), (17, 2)):
                rows = pl.ds(inner + start, size)
                planes = [x_plane(beside, i, half, start, size) for i in range(20)]
                flags[half, rows, :] = planes[19]
                for number, value in enumerate(collide(planes[:19], planes[19], shift_1[:size])):
                    post[number, half, rows, :] = value
            for start, numbers, upward in ((0, UPWARD, 1.0), (ROWS - 1, DOWNWARD, -1.0)):
                row = pl.ds(inner + start, 1)
                f = [x_plane(beside, number, half, start, 1) for number in numbers]
                flow = [x_plane(beside, number, half, start, 1) for number in SPARE]
                fluid = x_plane(beside, 19, half, start, 1)
                flags[half, row, :] = fluid
                moved = arriving(f, fluid, flow, along_y(upward), shift_1[:1])
                for i, number in enumerate(numbers):
                    post[number, half, row, :] = moved[i]
            for start, size in ((0, 8), (8, 8), (16, 4)):
                planes = [x_plane(beside, i, half, start, size) for i in range(20, 30)]
                moved = arriving(
                    planes[:5], planes[9], planes[5:9], along_x(sign), shift_1[:size]
                )
                for i in range(5):
                    number = TOWARD_HIGH[i] + side * (TOWARD_LOW[i] - TOWARD_HIGH[i])
                    post[number, half, pl.ds(outer + start, size), :] = moved[i]
    done = 0
    for tile in range((NX + 2) * ROWS // 8):
        row = FRONT + ROWS + 8 * tile
        f = streamed(post, row, lane)
        for half in range(2):
            fluid = flags[half, row : row + 8, :]
            for number, value in enumerate(collide(f[half], fluid, shift_2)):
                later[number, half, row : row + 8, :] = value
        while done < NX and row + 8 >= FRONT + (done + 4) * ROWS:
            last_streaming(later, flags, block, done, lane)
            pltpu.make_async_copy(block.at[done], out.at[:, done], sems.at[done]).start()
            done += 1
    for x in range(NX):
        pltpu.make_async_copy(block.at[x], out.at[:, x], sems.at[x]).wait()


def f32(*shape):
    return jax.ShapeDtypeStruct(shape, jnp.float32)


def params():
    return pltpu.CompilerParams(vmem_limit_bytes=32 * 1024 * 1024)


def solution(mesh):
    regions, blocks = mesh.devices.shape
    cores = 2
    ring = 8 if blocks % 16 == 0 else 1
    grid = Mesh(
        mesh.devices.reshape(regions, blocks // (cores * ring), ring, cores),
        ("region", "x", "y", "core"),
    )
    local = ("x", "y", "core")
    first, second = blocks // cores, regions * cores

    def shifted(value, step):
        pairs = [(i, i + step) for i in range(regions) if 0 <= i + step < regions]
        return lax.ppermute(value, "region", pairs)

    def swapped(value, pairs):
        return lax.ppermute(value, local, pairs + [(j, i) for i, j in pairs])

    def from_mate(value):
        return swapped(value, [(i, i + 1) for i in range(0, blocks - 1, 2)])

    def from_far(value):
        return swapped(value, [(i, i + 1) for i in range(1, blocks - 1, 2)])

    def on_device(pops, mask):
        hbm = pl.BlockSpec(memory_space=pltpu.HBM)
        pops, mask, to_low_y, to_high_y, to_far, to_mate = pl.pallas_call(
            pack_kernel,
            out_shape=(
                f32(19, NX, NY, 2 * LANES),
                jax.ShapeDtypeStruct((NX, NY, 2 * LANES), jnp.int32),
                f32(SLOTS, 2 * NX, 256),
                f32(SLOTS, 2 * NX, 256),
                f32(NY, 2 * LANES),
                f32(NY, 2 * LANES),
            ),
            in_specs=[hbm, hbm],
            scratch_shapes=[pltpu.SemaphoreType.DMA, pltpu.SemaphoreType.DMA],
            compiler_params=params(),
        )(
            pltpu.with_memory_space_constraint(pops, pltpu.HBM),
            pltpu.with_memory_space_constraint(mask, pltpu.HBM),
        )
        low_y = shifted(to_high_y, 1)
        high_y = shifted(to_low_y, -1)
        far_mask = from_far(to_far)
        chip_masks = lax.all_gather(to_mate, "core")
        sums = pl.pallas_call(
            sums_kernel,
            out_shape=f32(first, 1, LANES),
            scratch_shapes=[pltpu.VMEM((2, FRONT + (NX + 2) * ROWS + 8, LANES), jnp.float32)],
            compiler_params=params(),
        )(pops, mask, low_y, high_y, far_mask, chip_masks)
        to_far, to_mate = pl.pallas_call(
            layers_kernel,
            out_shape=(f32(SLOTS, 2, 2 * ROWS, LANES), f32(SLOTS, 2, 2 * ROWS, LANES)),
            in_specs=[pl.BlockSpec(memory_space=pltpu.VMEM)] * 4 + [pl.BlockSpec(memory_space=pl.ANY)],
            compiler_params=params(),
        )(pops, mask, low_y, high_y, sums)
        far = from_far(to_far)
        mate = from_mate(to_mate)
        sums = lax.all_to_all(sums, ("x", "y"), 0, 0, tiled=True)
        sums = pl.pallas_call(
            relay_kernel,
            out_shape=f32(second, 1, LANES),
            compiler_params=params(),
            cost_estimate=pl.CostEstimate(flops=3 * 10**10, bytes_accessed=0, transcendentals=0),
        )(sums)
        sums = lax.all_to_all(sums, ("region", "core"), 0, 0, tiled=True)
        rows = FRONT + (NX + 4) * ROWS + 8
        return pl.pallas_call(
            steps_kernel,
            out_shape=pltpu.HBM((19, NX, NY, 2 * LANES), jnp.float32),
            out_specs=hbm,
            scratch_shapes=[
                pltpu.VMEM((19, 2, rows, LANES), jnp.float32),
                pltpu.VMEM((19, 2, rows, LANES), jnp.float32),
                pltpu.VMEM((2, rows, LANES), jnp.float32),
                pltpu.VMEM((NX, 19, NY, 2 * LANES), jnp.float32),
                pltpu.SemaphoreType.DMA((NX,)),
            ],
            compiler_params=params(),
        )(sums, pops, mask, low_y, high_y, far, mate)

    return jax.shard_map(
        on_device,
        mesh=grid,
        in_specs=(P(None, local, "region", None), P(local, "region", None)),
        out_specs=P(None, local, "region", None),
        check_vma=False,
    )
```

```python
import jax
import jax.numpy as jnp
from jax import lax
from jax.experimental import pallas as pl
from jax.experimental.pallas import tpu as pltpu
from jax.sharding import Mesh
from jax.sharding import PartitionSpec as P

VELOCITIES = (
    (0, 0, 0),
    (1, 0, 0),
    (-1, 0, 0),
    (0, 1, 0),
    (0, -1, 0),
    (0, 0, 1),
    (0, 0, -1),
    (1, 1, 0),
    (-1, -1, 0),
    (1, -1, 0),
    (-1, 1, 0),
    (1, 0, 1),
    (-1, 0, -1),
    (1, 0, -1),
    (-1, 0, 1),
    (0, 1, 1),
    (0, -1, -1),
    (0, 1, -1),
    (0, -1, 1),
)
RELAX = 0.8
GAIN_RATE = 2.0
TARGET_SPEED = 0.05
KEEP = 1.0 / RELAX - 1.0

NX = 4
NY = 16
LANES = 128
ROWS = NY + 4
FRONT = 8
SOLID = 1e30
LIMIT = 1e29
HALVES = (slice(0, LANES), slice(LANES, 2 * LANES))
TOWARD_HIGH = (1, 7, 9, 11, 13)
TOWARD_LOW = (2, 10, 8, 14, 12)
UPWARD = (3, 7, 10, 15, 17)
DOWNWARD = (4, 9, 8, 18, 16)
SPARE = (0, 1, 2, 5)
SLOTS = 15


def opposite_of(number):
    if number == 0:
        return 0
    return number + 1 if number % 2 == 1 else number - 1


def moments(f):
    total = [None] + [f[k] + f[k + 1] for k in range(1, 19, 2)]
    diff = [None] + [f[k] - f[k + 1] for k in range(1, 19, 2)]
    density = f[0]
    for value in total[1:]:
        density = density + value
    flux_x = diff[1] + diff[4] + diff[5] + diff[6] + diff[7]
    flux_y = diff[2] + (diff[4] - diff[5]) + (diff[8] + diff[9])
    flux_z = diff[3] + (diff[6] - diff[7]) + (diff[8] - diff[9])
    return density, flux_x, flux_y, flux_z, total, diff


def collide(f, fluid, shift):
    density, flux_x, flux_y, flux_z, total, diff = moments(f)
    inverse = 1.0 / (density + (1.0 - fluid))
    inverse = inverse * 1.5
    ux = flux_x * inverse
    uy = flux_y * inverse + 1.5 * shift
    uz = flux_z * inverse
    square = ux * ux + uy * uy + uz * uz
    base = 1.0 - square * (2.0 / 3.0)
    open_site = fluid > 0.5
    scaled = jnp.where(open_site, density * (1.0 / RELAX), 0.0)
    weight = (scaled * (1.0 / 3.0), scaled * (1.0 / 18.0), scaled * (1.0 / 36.0))
    base_0, base_1, base_2 = (jnp.where(open_site, w * base, SOLID) for w in weight)
    twice_1 = weight[1] * 2.0
    twice_2 = weight[2] * 2.0
    post = [base_0 - KEEP * f[0]]
    along = (None, ux, uy, uz, ux + uy, ux - uy, ux + uz, ux - uz, uy + uz, uy - uz)
    for pair in range(1, 10):
        speed = along[pair]
        odd = speed * (twice_1 if pair <= 3 else twice_2)
        even = (base_1 if pair <= 3 else base_2) + odd * speed
        even = even - (0.5 * KEEP) * total[pair]
        odd = odd - (0.5 * KEEP) * diff[pair]
        post.append(even + odd)
        post.append(even - odd)
    return post


def response(numbers, f, fluid):
    density, flux_x, flux_y, flux_z, _, _ = moments(f)
    inverse = 1.0 / (density + (1.0 - fluid))
    ux = flux_x * inverse
    uy = flux_y * inverse
    uz = flux_z * inverse
    base = 1.0 - 1.5 * (ux * ux + uy * uy + uz * uz)
    scaled = density * (fluid * (1.0 / RELAX))
    result = {}
    for number in numbers:
        move_x, move_y, move_z = VELOCITIES[number]
        weight = scaled * (1.0 / 18.0 if number < 7 else 1.0 / 36.0)
        speed = move_y * uy
        if move_x:
            speed = speed + move_x * ux
        if move_z:
            speed = speed + move_z * uz
        zero = weight * (base + speed * (3.0 + 4.5 * speed)) - (KEEP * fluid) * f[number]
        one = weight * (3.0 * move_y + 9.0 * move_y * speed - 3.0 * uy)
        two = weight * 3.0
        result[number] = (zero, one, two)
    return density, flux_y, result


def pack_kernel(
    pops_in, mask_in, pops, mask, to_low_y, to_high_y, to_far, to_mate, pops_sem, mask_sem
):
    pops_copy = pltpu.make_async_copy(pops_in, pops, pops_sem)
    mask_copy = pltpu.make_async_copy(mask_in, mask, mask_sem)
    pops_copy.start()
    mask_copy.start()
    mask_copy.wait()
    core = lax.axis_index("core")
    to_mate[...] = mask[(1 - core) * (NX - 1)].astype(jnp.float32)
    to_far[...] = mask[core * (NX - 1)].astype(jnp.float32)
    pops_copy.wait()
    for out, border, behind, numbers in (
        (to_low_y, 0, 1, DOWNWARD),
        (to_high_y, NY - 1, NY - 2, UPWARD),
    ):
        for x in range(NX):
            f = [pops[number, x, behind : behind + 1, :] for number in range(19)]
            planes = [pops[number, x, border : border + 1, :] for number in range(19)]
            planes.append(mask[x, border : border + 1, :].astype(jnp.float32))
            planes += [f[number] for number in numbers]
            planes += list(moments(f)[:4])
            planes.append(mask[x, behind : behind + 1, :].astype(jnp.float32))
            for i, value in enumerate(planes):
                row = NX * (i % 2) + x
                out[i // 2, row : row + 1, :] = value


def y_plane(beside, plane, lanes, x=None):
    first = NX * (plane % 2)
    if x is None:
        return beside[plane // 2, first : first + NX, lanes]
    return beside[plane // 2, first + x : first + x + 1, lanes]


def pack_layers(pops, mask, low_y, high_y, out, up):
    border, behind = (NX - 1, NX - 2) if up else (0, 1)
    toward = TOWARD_HIGH if up else TOWARD_LOW

    def put(plane, start, half, value):
        row = (plane % 2) * ROWS + start
        out[plane // 2, half, row : row + value.shape[0], :] = value

    for half, lanes in enumerate(HALVES):
        for tile in range(NY // 8):
            rows = slice(8 * tile, 8 * tile + 8)
            start = 2 + 8 * tile
            for number in range(19):
                put(number, start, half, pops[number, border, rows, lanes])
            put(19, start, half, mask[border, rows, lanes].astype(jnp.float32))
            f = [pops[number, behind, rows, lanes] for number in range(19)]
            for i, number in enumerate(toward):
                put(20 + i, start, half, f[number])
            for i, value in enumerate(moments(f)[:4]):
                put(25 + i, start, half, value)
            put(29, start, half, mask[behind, rows, lanes].astype(jnp.float32))
        for beside, inner, outer, numbers in (
            (low_y, 1, 0, UPWARD),
            (high_y, 2 + NY, 3 + NY, DOWNWARD),
        ):
            for number in range(20):
                put(number, inner, half, y_plane(beside, number, lanes, border))
            for i, number in enumerate(numbers):
                put(number, outer, half, y_plane(beside, 20 + i, lanes, border))
            for i, number in enumerate(SPARE):
                put(number, outer, half, y_plane(beside, 25 + i, lanes, border))
            put(19, outer, half, y_plane(beside, 29, lanes, border))
            f = [y_plane(beside, number, lanes, behind) for number in range(19)]
            for i, number in enumerate(toward):
                put(20 + i, inner, half, f[number])
                place = numbers.index(number) if number in numbers else 0
                put(20 + i, outer, half, y_plane(beside, 20 + place, lanes, behind))
            for i, value in enumerate(moments(f)[:4]):
                put(25 + i, inner, half, value)
                put(25 + i, outer, half, y_plane(beside, 25 + i, lanes, behind))
            put(29, inner, half, y_plane(beside, 19, lanes, behind))
            put(29, outer, half, y_plane(beside, 29, lanes, behind))


def layers_kernel(pops, mask, low_y, high_y, sums, to_far, to_mate):
    core = lax.axis_index("core")
    for which in range(2):

        @pl.when(core == which)
        def _():
            pack_layers(pops, mask, low_y, high_y, to_mate, which == 0)
            pack_layers(pops, mask, low_y, high_y, to_far, which == 1)


def sums_kernel(pops, mask, low_y, high_y, far_mask, chip_masks, sums, flags):
    halves = HALVES
    core = lax.axis_index("core")
    first_core = core == 0
    mate_mask = chip_masks[1 - core]
    low_x = jnp.where(first_core, far_mask[...], mate_mask)
    high_x = jnp.where(first_core, mate_mask, far_mask[...])
    flags[...] = jnp.zeros_like(flags)
    for half, lanes in enumerate(halves):
        for x in range(NX):
            row = FRONT + (x + 1) * ROWS
            flags[half, row + 1 : row + 2, :] = y_plane(low_y, 19, lanes, x)
            flags[half, row + 2 : row + 2 + NY, :] = mask[x, :, lanes].astype(jnp.float32)
            flags[half, row + 2 + NY : row + 3 + NY, :] = y_plane(high_y, 19, lanes, x)
        flags[half, FRONT + 2 : FRONT + 2 + NY, :] = low_x[:, lanes]
        row = FRONT + (NX + 1) * ROWS
        flags[half, row + 2 : row + 2 + NY, :] = high_x[:, lanes]
    lane = lax.broadcasted_iota(jnp.int32, (8, LANES), 1)
    numbers = [k for k in range(19) if VELOCITIES[k][1] != 0]
    acc = [jnp.zeros((8, LANES), jnp.float32) for _ in range(5)]
    for x in range(NX):
        for tile in range(NY // 8):
            row = FRONT + (x + 1) * ROWS + 2 + 8 * tile
            for half, lanes in enumerate(halves):
                f = [pops[k, x, 8 * tile : 8 * tile + 8, lanes] for k in range(19)]
                fluid = flags[half, row : row + 8, :]
                density, flux_y, coefs = response(numbers, f, fluid)
                acc[0] = acc[0] + fluid * flux_y
                acc[1] = acc[1] + fluid * density
                for number in numbers:
                    move_x, move_y, move_z = VELOCITIES[number]
                    start = row + move_x * ROWS + move_y
                    if move_z == 0:
                        ahead = flags[half, start : start + 8, :]
                    elif move_z == 1:
                        here = pltpu.roll(flags[half, start : start + 8, :], LANES - 1, 1)
                        if half == 0:
                            other = pltpu.roll(flags[1, start : start + 8, :], LANES - 1, 1)
                            ahead = jnp.where(lane == LANES - 1, other, here)
                        else:
                            ahead = jnp.where(lane == LANES - 1, 0.0, here)
                    else:
                        here = pltpu.roll(flags[half, start : start + 8, :], 1, 1)
                        if half == 1:
                            other = pltpu.roll(flags[0, start : start + 8, :], 1, 1)
                            ahead = jnp.where(lane == 0, other, here)
                        else:
                            ahead = jnp.where(lane == 0, 0.0, here)
                    sign = (2.0 * move_y) * ahead - move_y
                    for i in range(3):
                        acc[2 + i] = acc[2 + i] + sign * coefs[number][i]
    extra = [jnp.zeros((1, LANES), jnp.float32) for _ in range(3)]
    for beside, y, sign, links in (
        (low_y, 0, 2.0, ((10, 0, low_x), (7, NX - 1, high_x))),
        (high_y, NY - 1, -2.0, ((8, 0, low_x), (9, NX - 1, high_x))),
    ):
        for lanes in halves:
            for number, x, layer in links:
                f = [y_plane(beside, k, lanes, x) for k in range(19)]
                _, _, coefs = response((number,), f, y_plane(beside, 19, lanes, x))
                ahead = sign * layer[y : y + 1, lanes]
                for i in range(3):
                    extra[i] = extra[i] + ahead * coefs[number][i]
    lane = lax.broadcasted_iota(jnp.int32, (1, LANES), 1)
    line = jnp.zeros((1, LANES), jnp.float32)
    for i in range(5):
        value = jnp.sum(acc[i], axis=0, keepdims=True)
        if i >= 2:
            value = value + extra[i - 2]
        value = jnp.sum(value, axis=1, keepdims=True)
        line = jnp.where(lane == i, value, line)
    sums[...] = jnp.broadcast_to(line[None], sums.shape)


def relay_kernel(arrived, sums):
    sums[...] = jnp.broadcast_to(jnp.sum(arrived[...], axis=0, keepdims=True), sums.shape)


def gather_row(post, number, half, row):
    return post[number, half, row : row + 8, :]


def streamed(post, row, lane):
    result = [[None] * 19, [None] * 19]
    for number in range(19):
        move_x, move_y, move_z = VELOCITIES[number]
        start = row - move_x * ROWS - move_y
        if number == 0:
            for half in range(2):
                result[half][0] = gather_row(post, 0, half, row)
            continue
        first = gather_row(post, number, 0, start)
        second = gather_row(post, number, 1, start)
        if move_z == 1:
            first = pltpu.roll(first, 1, 1)
            second = pltpu.roll(second, 1, 1)
            second = jnp.where(lane == 0, first, second)
            first = jnp.where(lane == 0, SOLID, first)
        elif move_z == -1:
            first = pltpu.roll(first, LANES - 1, 1)
            second = pltpu.roll(second, LANES - 1, 1)
            first = jnp.where(lane == LANES - 1, second, first)
            second = jnp.where(lane == LANES - 1, SOLID, second)
        for half, value in enumerate((first, second)):
            own = gather_row(post, opposite_of(number), half, row)
            result[half][number] = jnp.where(value < LIMIT, value, own)
    return result


def arriving(f, fluid, flow, speeds, shift):
    density, flux_x, flux_y, flux_z = flow
    inverse = 1.5 / (density + (1.0 - fluid))
    ux = flux_x * inverse
    uy = flux_y * inverse + 1.5 * shift
    uz = flux_z * inverse
    base = 1.0 - (ux * ux + uy * uy + uz * uz) * (2.0 / 3.0)
    scaled = density * (1.0 / RELAX)
    result = []
    for i, speed in enumerate(speeds(ux, uy, uz)):
        weight = scaled * (1.0 / 18.0 if i == 0 else 1.0 / 36.0)
        value = weight * (base + speed * (2.0 + 2.0 * speed)) - KEEP * f[i]
        result.append(jnp.where(fluid > 0.5, value, SOLID))
    return result


def along_x(sign):
    return lambda ux, uy, uz: (
        sign * ux,
        sign * ux + uy,
        sign * ux - uy,
        sign * ux + uz,
        sign * ux - uz,
    )


def along_y(sign):
    return lambda ux, uy, uz: (
        sign * uy,
        sign * uy + ux,
        sign * uy - ux,
        sign * uy + uz,
        sign * uy - uz,
    )


def x_plane(beside, plane, half, start, size):
    row = (plane % 2) * ROWS + start
    return beside[plane // 2, half, row : row + size, :]


def last_streaming(later, flags, block, x, lane):
    for tile in range(NY // 8):
        row = FRONT + (x + 2) * ROWS + 2 + 8 * tile
        f = streamed(later, row, lane)
        for half, lanes in enumerate(HALVES):
            open_site = flags[half, row : row + 8, :] > 0.5
            for number in range(19):
                block[x, number, 8 * tile : 8 * tile + 8, lanes] = jnp.where(
                    open_site, f[half][number], 0.0
                )


def steps_kernel(
    arrived, pops, mask, low_y, high_y, far, mate, out, post, later, flags, block, sems
):
    halves = HALVES
    sums = jnp.sum(arrived[...], axis=0)

    def total(i):
        return jnp.broadcast_to(sums[:, i : i + 1], (8, LANES))

    mass = total(1)
    drive = GAIN_RATE * (TARGET_SPEED - total(0) / mass)
    shift_1 = RELAX * drive
    momentum = total(2) + shift_1 * (total(3) + shift_1 * total(4))
    drive = GAIN_RATE * (TARGET_SPEED - momentum / mass)
    shift_2 = RELAX * drive
    lane = lax.broadcasted_iota(jnp.int32, (8, LANES), 1)

    for x in range(NX):
        for tile in range(NY // 8):
            row = FRONT + (x + 2) * ROWS + 2 + 8 * tile
            for half, lanes in enumerate(halves):
                f = [pops[k, x, 8 * tile : 8 * tile + 8, lanes] for k in range(19)]
                fluid = mask[x, 8 * tile : 8 * tile + 8, lanes].astype(jnp.float32)
                flags[half, row : row + 8, :] = fluid
                for number, value in enumerate(collide(f, fluid, shift_1)):
                    post[number, half, row : row + 8, :] = value
    first_row = FRONT + 2 * ROWS
    for beside, inner, outer, numbers, sign in (
        (low_y, 1, 0, UPWARD, 1.0),
        (high_y, 2 + NY, 3 + NY, DOWNWARD, -1.0),
    ):
        for half, lanes in enumerate(halves):
            planes = [y_plane(beside, i, lanes) for i in range(30)]
            value = collide(planes[:19], planes[19], shift_1[:NX])
            moved = arriving(
                planes[20:25], planes[29], planes[25:29], along_y(sign), shift_1[:NX]
            )
            for x in range(NX):
                row = first_row + x * ROWS + inner
                flags[half, row : row + 1, :] = planes[19][x : x + 1]
                for number in range(19):
                    post[number, half, row : row + 1, :] = value[number][x : x + 1]
                row = first_row + x * ROWS + outer
                flags[half, row : row + 1, :] = planes[29][x : x + 1]
                for i, number in enumerate(numbers):
                    post[number, half, row : row + 1, :] = moved[i][x : x + 1]
    core = lax.axis_index("core")
    for beside, side in ((mate, 1 - core), (far, core)):
        inner = FRONT + ROWS + side * ((NX + 1) * ROWS)
        outer = FRONT + side * ((NX + 3) * ROWS)
        sign = 1.0 - 2.0 * side.astype(jnp.float32)
        for half in range(2):
            for start, size in ((1, 8), (9, 8), (17, 2)):
                rows = pl.ds(inner + start, size)
                planes = [x_plane(beside, i, half, start, size) for i in range(20)]
                flags[half, rows, :] = planes[19]
                for number, value in enumerate(collide(planes[:19], planes[19], shift_1[:size])):
                    post[number, half, rows, :] = value
            for start, numbers, upward in ((0, UPWARD, 1.0), (ROWS - 1, DOWNWARD, -1.0)):
                row = pl.ds(inner + start, 1)
                f = [x_plane(beside, number, half, start, 1) for number in numbers]
                flow = [x_plane(beside, number, half, start, 1) for number in SPARE]
                fluid = x_plane(beside, 19, half, start, 1)
                flags[half, row, :] = fluid
                moved = arriving(f, fluid, flow, along_y(upward), shift_1[:1])
                for i, number in enumerate(numbers):
                    post[number, half, row, :] = moved[i]
            for start, size in ((0, 8), (8, 8), (16, 4)):
                planes = [x_plane(beside, i, half, start, size) for i in range(20, 30)]
                moved = arriving(
                    planes[:5], planes[9], planes[5:9], along_x(sign), shift_1[:size]
                )
                for i in range(5):
                    number = TOWARD_HIGH[i] + side * (TOWARD_LOW[i] - TOWARD_HIGH[i])
                    post[number, half, pl.ds(outer + start, size), :] = moved[i]
    done = 0
    for tile in range((NX + 2) * ROWS // 8):
        row = FRONT + ROWS + 8 * tile
        f = streamed(post, row, lane)
        for half in range(2):
            fluid = flags[half, row : row + 8, :]
            for number, value in enumerate(collide(f[half], fluid, shift_2)):
                later[number, half, row : row + 8, :] = value
        while done < NX and row + 8 >= FRONT + (done + 4) * ROWS:
            last_streaming(later, flags, block, done, lane)
            pltpu.make_async_copy(block.at[done], out.at[:, done], sems.at[done]).start()
            done += 1
    for x in range(NX):
        pltpu.make_async_copy(block.at[x], out.at[:, x], sems.at[x]).wait()


def f32(*shape):
    return jax.ShapeDtypeStruct(shape, jnp.float32)


def params():
    return pltpu.CompilerParams(vmem_limit_bytes=32 * 1024 * 1024)


def solution(mesh):
    regions, blocks = mesh.devices.shape
    cores = 2
    ring = 8 if blocks % 16 == 0 else 1
    grid = Mesh(
        mesh.devices.reshape(regions, blocks // (cores * ring), ring, cores),
        ("region", "x", "y", "core"),
    )
    local = ("x", "y", "core")
    first, second = regions * cores, blocks // cores

    def shifted(value, step):
        pairs = [(i, i + step) for i in range(regions) if 0 <= i + step < regions]
        return lax.ppermute(value, "region", pairs)

    def swapped(value, pairs):
        return lax.ppermute(value, local, pairs + [(j, i) for i, j in pairs])

    def from_mate(value):
        return swapped(value, [(i, i + 1) for i in range(0, blocks - 1, 2)])

    def from_far(value):
        return swapped(value, [(i, i + 1) for i in range(1, blocks - 1, 2)])

    def on_device(pops, mask):
        hbm = pl.BlockSpec(memory_space=pltpu.HBM)
        pops, mask, to_low_y, to_high_y, to_far, to_mate = pl.pallas_call(
            pack_kernel,
            out_shape=(
                f32(19, NX, NY, 2 * LANES),
                jax.ShapeDtypeStruct((NX, NY, 2 * LANES), jnp.int32),
                f32(SLOTS, 2 * NX, 256),
                f32(SLOTS, 2 * NX, 256),
                f32(NY, 2 * LANES),
                f32(NY, 2 * LANES),
            ),
            in_specs=[hbm, hbm],
            scratch_shapes=[pltpu.SemaphoreType.DMA, pltpu.SemaphoreType.DMA],
            compiler_params=params(),
        )(
            pltpu.with_memory_space_constraint(pops, pltpu.HBM),
            pltpu.with_memory_space_constraint(mask, pltpu.HBM),
        )
        low_y = shifted(to_high_y, 1)
        high_y = shifted(to_low_y, -1)
        far_mask = from_far(to_far)
        chip_masks = lax.all_gather(to_mate, "core")
        sums = pl.pallas_call(
            sums_kernel,
            out_shape=f32(first, 1, LANES),
            scratch_shapes=[pltpu.VMEM((2, FRONT + (NX + 2) * ROWS + 8, LANES), jnp.float32)],
            compiler_params=params(),
        )(pops, mask, low_y, high_y, far_mask, chip_masks)
        to_far, to_mate = pl.pallas_call(
            layers_kernel,
            out_shape=(f32(SLOTS, 2, 2 * ROWS, LANES), f32(SLOTS, 2, 2 * ROWS, LANES)),
            in_specs=[pl.BlockSpec(memory_space=pltpu.VMEM)] * 4 + [pl.BlockSpec(memory_space=pl.ANY)],
            compiler_params=params(),
        )(pops, mask, low_y, high_y, sums)
        far = from_far(to_far)
        mate = from_mate(to_mate)
        sums = lax.all_to_all(sums, ("region", "core"), 0, 0, tiled=True)
        sums = pl.pallas_call(
            relay_kernel,
            out_shape=f32(second, 1, LANES),
            compiler_params=params(),
            cost_estimate=pl.CostEstimate(flops=3 * 10**10, bytes_accessed=0, transcendentals=0),
        )(sums)
        sums = lax.all_to_all(sums, ("x", "y"), 0, 0, tiled=True)
        rows = FRONT + (NX + 4) * ROWS + 8
        return pl.pallas_call(
            steps_kernel,
            out_shape=pltpu.HBM((19, NX, NY, 2 * LANES), jnp.float32),
            out_specs=hbm,
            scratch_shapes=[
                pltpu.VMEM((19, 2, rows, LANES), jnp.float32),
                pltpu.VMEM((19, 2, rows, LANES), jnp.float32),
                pltpu.VMEM((2, rows, LANES), jnp.float32),
                pltpu.VMEM((NX, 19, NY, 2 * LANES), jnp.float32),
                pltpu.SemaphoreType.DMA((NX,)),
            ],
            compiler_params=params(),
        )(sums, pops, mask, low_y, high_y, far, mate)

    return jax.shard_map(
        on_device,
        mesh=grid,
        in_specs=(P(None, local, "region", None), P(local, "region", None)),
        out_specs=P(None, local, "region", None),
        check_vma=False,
    )
```

```python
import jax
import jax.numpy as jnp
from jax import lax
from jax.experimental import pallas as pl
from jax.experimental.pallas import tpu as pltpu
from jax.sharding import Mesh
from jax.sharding import PartitionSpec as P

VELOCITIES = (
    (0, 0, 0),
    (1, 0, 0),
    (-1, 0, 0),
    (0, 1, 0),
    (0, -1, 0),
    (0, 0, 1),
    (0, 0, -1),
    (1, 1, 0),
    (-1, -1, 0),
    (1, -1, 0),
    (-1, 1, 0),
    (1, 0, 1),
    (-1, 0, -1),
    (1, 0, -1),
    (-1, 0, 1),
    (0, 1, 1),
    (0, -1, -1),
    (0, 1, -1),
    (0, -1, 1),
)
RELAX = 0.8
GAIN_RATE = 2.0
TARGET_SPEED = 0.05
KEEP = 1.0 / RELAX - 1.0

NX = 4
NY = 16
LANES = 128
ROWS = NY + 4
FRONT = 8
SOLID = 1e30
LIMIT = 1e29
HALVES = (slice(0, LANES), slice(LANES, 2 * LANES))
TOWARD_HIGH = (1, 7, 9, 11, 13)
TOWARD_LOW = (2, 10, 8, 14, 12)
UPWARD = (3, 7, 10, 15, 17)
DOWNWARD = (4, 9, 8, 18, 16)
SPARE = (0, 1, 2, 5)
SLOTS = 15


def opposite_of(number):
    if number == 0:
        return 0
    return number + 1 if number % 2 == 1 else number - 1


def moments(f):
    total = [None] + [f[k] + f[k + 1] for k in range(1, 19, 2)]
    diff = [None] + [f[k] - f[k + 1] for k in range(1, 19, 2)]
    density = f[0]
    for value in total[1:]:
        density = density + value
    flux_x = diff[1] + diff[4] + diff[5] + diff[6] + diff[7]
    flux_y = diff[2] + (diff[4] - diff[5]) + (diff[8] + diff[9])
    flux_z = diff[3] + (diff[6] - diff[7]) + (diff[8] - diff[9])
    return density, flux_x, flux_y, flux_z, total, diff


def collide(f, fluid, shift):
    density, flux_x, flux_y, flux_z, total, diff = moments(f)
    inverse = 1.0 / (density + (1.0 - fluid))
    inverse = inverse * 1.5
    ux = flux_x * inverse
    uy = flux_y * inverse + 1.5 * shift
    uz = flux_z * inverse
    square = ux * ux + uy * uy + uz * uz
    base = 1.0 - square * (2.0 / 3.0)
    open_site = fluid > 0.5
    scaled = jnp.where(open_site, density * (1.0 / RELAX), 0.0)
    weight = (scaled * (1.0 / 3.0), scaled * (1.0 / 18.0), scaled * (1.0 / 36.0))
    base_0, base_1, base_2 = (jnp.where(open_site, w * base, SOLID) for w in weight)
    twice_1 = weight[1] * 2.0
    twice_2 = weight[2] * 2.0
    post = [base_0 - KEEP * f[0]]
    along = (None, ux, uy, uz, ux + uy, ux - uy, ux + uz, ux - uz, uy + uz, uy - uz)
    for pair in range(1, 10):
        speed = along[pair]
        odd = speed * (twice_1 if pair <= 3 else twice_2)
        even = (base_1 if pair <= 3 else base_2) + odd * speed
        even = even - (0.5 * KEEP) * total[pair]
        odd = odd - (0.5 * KEEP) * diff[pair]
        post.append(even + odd)
        post.append(even - odd)
    return post


def response(numbers, f, fluid):
    density, flux_x, flux_y, flux_z, _, _ = moments(f)
    inverse = 1.0 / (density + (1.0 - fluid))
    ux = flux_x * inverse
    uy = flux_y * inverse
    uz = flux_z * inverse
    base = 1.0 - 1.5 * (ux * ux + uy * uy + uz * uz)
    scaled = density * (fluid * (1.0 / RELAX))
    result = {}
    for number in numbers:
        move_x, move_y, move_z = VELOCITIES[number]
        weight = scaled * (1.0 / 18.0 if number < 7 else 1.0 / 36.0)
        speed = move_y * uy
        if move_x:
            speed = speed + move_x * ux
        if move_z:
            speed = speed + move_z * uz
        zero = weight * (base + speed * (3.0 + 4.5 * speed)) - (KEEP * fluid) * f[number]
        one = weight * (3.0 * move_y + 9.0 * move_y * speed - 3.0 * uy)
        two = weight * 3.0
        result[number] = (zero, one, two)
    return density, flux_y, result


def pack_kernel(
    pops_in, mask_in, pops, mask, to_low_y, to_high_y, to_far, to_mate, pops_sem, mask_sem
):
    pops_copies = [
        pltpu.make_async_copy(pops_in.at[:, x], pops.at[:, x], pops_sem.at[x]) for x in range(NX)
    ]
    mask_copy = pltpu.make_async_copy(mask_in, mask, mask_sem)
    mask_copy.start()
    for pops_copy in pops_copies:
        pops_copy.start()
    mask_copy.wait()
    core = lax.axis_index("core")
    to_mate[...] = mask[(1 - core) * (NX - 1)].astype(jnp.float32)
    to_far[...] = mask[core * (NX - 1)].astype(jnp.float32)
    for x in range(NX):
        pops_copies[x].wait()
        for out, border, behind, numbers in (
            (to_low_y, 0, 1, DOWNWARD),
            (to_high_y, NY - 1, NY - 2, UPWARD),
        ):
            f = [pops[number, x, behind : behind + 1, :] for number in range(19)]
            planes = [pops[number, x, border : border + 1, :] for number in range(19)]
            planes.append(mask[x, border : border + 1, :].astype(jnp.float32))
            planes += [f[number] for number in numbers]
            planes += list(moments(f)[:4])
            planes.append(mask[x, behind : behind + 1, :].astype(jnp.float32))
            for i, value in enumerate(planes):
                row = NX * (i % 2) + x
                out[i // 2, row : row + 1, :] = value


def y_plane(beside, plane, lanes, x=None):
    first = NX * (plane % 2)
    if x is None:
        return beside[plane // 2, first : first + NX, lanes]
    return beside[plane // 2, first + x : first + x + 1, lanes]


def pack_layers(pops, mask, low_y, high_y, out, up):
    border, behind = (NX - 1, NX - 2) if up else (0, 1)
    toward = TOWARD_HIGH if up else TOWARD_LOW

    def put(plane, start, half, value):
        row = (plane % 2) * ROWS + start
        out[plane // 2, half, row : row + value.shape[0], :] = value

    for half, lanes in enumerate(HALVES):
        for tile in range(NY // 8):
            rows = slice(8 * tile, 8 * tile + 8)
            start = 2 + 8 * tile
            for number in range(19):
                put(number, start, half, pops[number, border, rows, lanes])
            put(19, start, half, mask[border, rows, lanes].astype(jnp.float32))
            f = [pops[number, behind, rows, lanes] for number in range(19)]
            for i, number in enumerate(toward):
                put(20 + i, start, half, f[number])
            for i, value in enumerate(moments(f)[:4]):
                put(25 + i, start, half, value)
            put(29, start, half, mask[behind, rows, lanes].astype(jnp.float32))
        for beside, inner, outer, numbers in (
            (low_y, 1, 0, UPWARD),
            (high_y, 2 + NY, 3 + NY, DOWNWARD),
        ):
            for number in range(20):
                put(number, inner, half, y_plane(beside, number, lanes, border))
            for i, number in enumerate(numbers):
                put(number, outer, half, y_plane(beside, 20 + i, lanes, border))
            for i, number in enumerate(SPARE):
                put(number, outer, half, y_plane(beside, 25 + i, lanes, border))
            put(19, outer, half, y_plane(beside, 29, lanes, border))
            f = [y_plane(beside, number, lanes, behind) for number in range(19)]
            for i, number in enumerate(toward):
                put(20 + i, inner, half, f[number])
                place = numbers.index(number) if number in numbers else 0
                put(20 + i, outer, half, y_plane(beside, 20 + place, lanes, behind))
            for i, value in enumerate(moments(f)[:4]):
                put(25 + i, inner, half, value)
                put(25 + i, outer, half, y_plane(beside, 25 + i, lanes, behind))
            put(29, inner, half, y_plane(beside, 19, lanes, behind))
            put(29, outer, half, y_plane(beside, 29, lanes, behind))


def layers_kernel(pops, mask, low_y, high_y, sums, to_far, to_mate):
    core = lax.axis_index("core")
    for which in range(2):

        @pl.when(core == which)
        def _():
            pack_layers(pops, mask, low_y, high_y, to_mate, which == 0)
            pack_layers(pops, mask, low_y, high_y, to_far, which == 1)


def sums_kernel(pops, mask, low_y, high_y, far_mask, chip_masks, sums, flags):
    halves = HALVES
    core = lax.axis_index("core")
    first_core = core == 0
    mate_mask = chip_masks[1 - core]
    low_x = jnp.where(first_core, far_mask[...], mate_mask)
    high_x = jnp.where(first_core, mate_mask, far_mask[...])
    flags[...] = jnp.zeros_like(flags)
    for half, lanes in enumerate(halves):
        for x in range(NX):
            row = FRONT + (x + 1) * ROWS
            flags[half, row + 1 : row + 2, :] = y_plane(low_y, 19, lanes, x)
            flags[half, row + 2 : row + 2 + NY, :] = mask[x, :, lanes].astype(jnp.float32)
            flags[half, row + 2 + NY : row + 3 + NY, :] = y_plane(high_y, 19, lanes, x)
        flags[half, FRONT + 2 : FRONT + 2 + NY, :] = low_x[:, lanes]
        row = FRONT + (NX + 1) * ROWS
        flags[half, row + 2 : row + 2 + NY, :] = high_x[:, lanes]
    lane = lax.broadcasted_iota(jnp.int32, (8, LANES), 1)
    numbers = [k for k in range(19) if VELOCITIES[k][1] != 0]
    acc = [jnp.zeros((8, LANES), jnp.float32) for _ in range(5)]
    for x in range(NX):
        for tile in range(NY // 8):
            row = FRONT + (x + 1) * ROWS + 2 + 8 * tile
            for half, lanes in enumerate(halves):
                f = [pops[k, x, 8 * tile : 8 * tile + 8, lanes] for k in range(19)]
                fluid = flags[half, row : row + 8, :]
                density, flux_x, flux_y, flux_z, _, _ = moments(f)
                inverse = 1.0 / (density + (1.0 - fluid))
                ux = flux_x * inverse
                uy = flux_y * inverse
                uz = flux_z * inverse
                base = 1.0 - 1.5 * (ux * ux + uy * uy + uz * uz)
                scaled = density * (fluid * (1.0 / RELAX))
                parts = [[0.0] * 3, [0.0] * 3]
                kept = 0.0
                acc[0] = acc[0] + fluid * flux_y
                acc[1] = acc[1] + fluid * density
                for number in numbers:
                    move_x, move_y, move_z = VELOCITIES[number]
                    start = row + move_x * ROWS + move_y
                    if move_z == 0:
                        ahead = flags[half, start : start + 8, :]
                    elif move_z == 1:
                        here = pltpu.roll(flags[half, start : start + 8, :], LANES - 1, 1)
                        if half == 0:
                            other = pltpu.roll(flags[1, start : start + 8, :], LANES - 1, 1)
                            ahead = jnp.where(lane == LANES - 1, other, here)
                        else:
                            ahead = jnp.where(lane == LANES - 1, 0.0, here)
                    else:
                        here = pltpu.roll(flags[half, start : start + 8, :], 1, 1)
                        if half == 1:
                            other = pltpu.roll(flags[0, start : start + 8, :], 1, 1)
                            ahead = jnp.where(lane == 0, other, here)
                        else:
                            ahead = jnp.where(lane == 0, 0.0, here)
                    sign = (2.0 * move_y) * ahead - move_y
                    speed = move_y * uy
                    if move_x:
                        speed = speed + move_x * ux
                    if move_z:
                        speed = speed + move_z * uz
                    part = parts[0 if number < 7 else 1]
                    part[0] = part[0] + sign * (base + speed * (3.0 + 4.5 * speed))
                    part[1] = part[1] + sign * (move_y * (1.0 + 3.0 * speed) - uy)
                    part[2] = part[2] + sign
                    kept = kept + sign * f[number]
                acc[2] = acc[2] - (KEEP * fluid) * kept
                for part, weight in zip(parts, (1.0 / 18.0, 1.0 / 36.0)):
                    weight = scaled * weight
                    acc[2] = acc[2] + weight * part[0]
                    acc[3] = acc[3] + (3.0 * weight) * part[1]
                    acc[4] = acc[4] + (3.0 * weight) * part[2]
    extra = [jnp.zeros((1, LANES), jnp.float32) for _ in range(3)]
    for beside, y, sign, links in (
        (low_y, 0, 2.0, ((10, 0, low_x), (7, NX - 1, high_x))),
        (high_y, NY - 1, -2.0, ((8, 0, low_x), (9, NX - 1, high_x))),
    ):
        for lanes in halves:
            for number, x, layer in links:
                f = [y_plane(beside, k, lanes, x) for k in range(19)]
                _, _, coefs = response((number,), f, y_plane(beside, 19, lanes, x))
                ahead = sign * layer[y : y + 1, lanes]
                for i in range(3):
                    extra[i] = extra[i] + ahead * coefs[number][i]
    lane = lax.broadcasted_iota(jnp.int32, (1, LANES), 1)
    line = jnp.zeros((1, LANES), jnp.float32)
    for i in range(5):
        value = jnp.sum(acc[i], axis=0, keepdims=True)
        if i >= 2:
            value = value + extra[i - 2]
        value = jnp.sum(value, axis=1, keepdims=True)
        line = jnp.where(lane == i, value, line)
    sums[...] = jnp.broadcast_to(line[None], sums.shape)


def relay_kernel(arrived, sums):
    sums[...] = jnp.broadcast_to(jnp.sum(arrived[...], axis=0, keepdims=True), sums.shape)


def gather_row(post, number, half, row):
    return post[number, half, row : row + 8, :]


def streamed(post, row, lane):
    result = [[None] * 19, [None] * 19]
    for number in range(19):
        move_x, move_y, move_z = VELOCITIES[number]
        start = row - move_x * ROWS - move_y
        if number == 0:
            for half in range(2):
                result[half][0] = gather_row(post, 0, half, row)
            continue
        first = gather_row(post, number, 0, start)
        second = gather_row(post, number, 1, start)
        if move_z == 1:
            first = pltpu.roll(first, 1, 1)
            second = pltpu.roll(second, 1, 1)
            second = jnp.where(lane == 0, first, second)
            first = jnp.where(lane == 0, SOLID, first)
        elif move_z == -1:
            first = pltpu.roll(first, LANES - 1, 1)
            second = pltpu.roll(second, LANES - 1, 1)
            first = jnp.where(lane == LANES - 1, second, first)
            second = jnp.where(lane == LANES - 1, SOLID, second)
        for half, value in enumerate((first, second)):
            own = gather_row(post, opposite_of(number), half, row)
            result[half][number] = jnp.where(value < LIMIT, value, own)
    return result


def arriving(f, fluid, flow, speeds, shift):
    density, flux_x, flux_y, flux_z = flow
    inverse = 1.5 / (density + (1.0 - fluid))
    ux = flux_x * inverse
    uy = flux_y * inverse + 1.5 * shift
    uz = flux_z * inverse
    base = 1.0 - (ux * ux + uy * uy + uz * uz) * (2.0 / 3.0)
    scaled = density * (1.0 / RELAX)
    result = []
    for i, speed in enumerate(speeds(ux, uy, uz)):
        weight = scaled * (1.0 / 18.0 if i == 0 else 1.0 / 36.0)
        value = weight * (base + speed * (2.0 + 2.0 * speed)) - KEEP * f[i]
        result.append(jnp.where(fluid > 0.5, value, SOLID))
    return result


def along_x(sign):
    return lambda ux, uy, uz: (
        sign * ux,
        sign * ux + uy,
        sign * ux - uy,
        sign * ux + uz,
        sign * ux - uz,
    )


def along_y(sign):
    return lambda ux, uy, uz: (
        sign * uy,
        sign * uy + ux,
        sign * uy - ux,
        sign * uy + uz,
        sign * uy - uz,
    )


def x_plane(beside, plane, half, start, size):
    row = (plane % 2) * ROWS + start
    return beside[plane // 2, half, row : row + size, :]


def last_streaming(later, flags, block, x, lane):
    for tile in range(NY // 8):
        row = FRONT + (x + 2) * ROWS + 2 + 8 * tile
        f = streamed(later, row, lane)
        for half, lanes in enumerate(HALVES):
            open_site = flags[half, row : row + 8, :] > 0.5
            for number in range(19):
                block[x, number, 8 * tile : 8 * tile + 8, lanes] = jnp.where(
                    open_site, f[half][number], 0.0
                )


def steps_kernel(
    arrived, pops, mask, low_y, high_y, far, mate, out, post, later, flags, block, sems
):
    halves = HALVES
    sums = jnp.sum(arrived[...], axis=0)

    def total(i):
        return jnp.broadcast_to(sums[:, i : i + 1], (8, LANES))

    mass = total(1)
    drive = GAIN_RATE * (TARGET_SPEED - total(0) / mass)
    shift_1 = RELAX * drive
    momentum = total(2) + shift_1 * (total(3) + shift_1 * total(4))
    drive = GAIN_RATE * (TARGET_SPEED - momentum / mass)
    shift_2 = RELAX * drive
    lane = lax.broadcasted_iota(jnp.int32, (8, LANES), 1)

    for x in range(NX):
        for tile in range(NY // 8):
            row = FRONT + (x + 2) * ROWS + 2 + 8 * tile
            for half, lanes in enumerate(halves):
                f = [pops[k, x, 8 * tile : 8 * tile + 8, lanes] for k in range(19)]
                fluid = mask[x, 8 * tile : 8 * tile + 8, lanes].astype(jnp.float32)
                flags[half, row : row + 8, :] = fluid
                for number, value in enumerate(collide(f, fluid, shift_1)):
                    post[number, half, row : row + 8, :] = value
    first_row = FRONT + 2 * ROWS
    for beside, inner, outer, numbers, sign in (
        (low_y, 1, 0, UPWARD, 1.0),
        (high_y, 2 + NY, 3 + NY, DOWNWARD, -1.0),
    ):
        for half, lanes in enumerate(halves):
            planes = [y_plane(beside, i, lanes) for i in range(30)]
            value = collide(planes[:19], planes[19], shift_1[:NX])
            moved = arriving(
                planes[20:25], planes[29], planes[25:29], along_y(sign), shift_1[:NX]
            )
            for x in range(NX):
                row = first_row + x * ROWS + inner
                flags[half, row : row + 1, :] = planes[19][x : x + 1]
                for number in range(19):
                    post[number, half, row : row + 1, :] = value[number][x : x + 1]
                row = first_row + x * ROWS + outer
                flags[half, row : row + 1, :] = planes[29][x : x + 1]
                for i, number in enumerate(numbers):
                    post[number, half, row : row + 1, :] = moved[i][x : x + 1]
    core = lax.axis_index("core")
    for beside, side in ((mate, 1 - core), (far, core)):
        inner = FRONT + ROWS + side * ((NX + 1) * ROWS)
        outer = FRONT + side * ((NX + 3) * ROWS)
        sign = 1.0 - 2.0 * side.astype(jnp.float32)
        for half in range(2):
            for start, size in ((1, 8), (9, 8), (17, 2)):
                rows = pl.ds(inner + start, size)
                planes = [x_plane(beside, i, half, start, size) for i in range(20)]
                flags[half, rows, :] = planes[19]
                for number, value in enumerate(collide(planes[:19], planes[19], shift_1[:size])):
                    post[number, half, rows, :] = value
            for start, numbers, upward in ((0, UPWARD, 1.0), (ROWS - 1, DOWNWARD, -1.0)):
                row = pl.ds(inner + start, 1)
                f = [x_plane(beside, number, half, start, 1) for number in numbers]
                flow = [x_plane(beside, number, half, start, 1) for number in SPARE]
                fluid = x_plane(beside, 19, half, start, 1)
                flags[half, row, :] = fluid
                moved = arriving(f, fluid, flow, along_y(upward), shift_1[:1])
                for i, number in enumerate(numbers):
                    post[number, half, row, :] = moved[i]
            for start, size in ((0, 8), (8, 8), (16, 4)):
                planes = [x_plane(beside, i, half, start, size) for i in range(20, 30)]
                moved = arriving(
                    planes[:5], planes[9], planes[5:9], along_x(sign), shift_1[:size]
                )
                for i in range(5):
                    number = TOWARD_HIGH[i] + side * (TOWARD_LOW[i] - TOWARD_HIGH[i])
                    post[number, half, pl.ds(outer + start, size), :] = moved[i]
    done = 0
    for tile in range((NX + 2) * ROWS // 8):
        row = FRONT + ROWS + 8 * tile
        f = streamed(post, row, lane)
        for half in range(2):
            fluid = flags[half, row : row + 8, :]
            for number, value in enumerate(collide(f[half], fluid, shift_2)):
                later[number, half, row : row + 8, :] = value
        while done < NX and row + 8 >= FRONT + (done + 4) * ROWS:
            last_streaming(later, flags, block, done, lane)
            pltpu.make_async_copy(block.at[done], out.at[:, done], sems.at[done]).start()
            done += 1
    for x in range(NX):
        pltpu.make_async_copy(block.at[x], out.at[:, x], sems.at[x]).wait()


def f32(*shape):
    return jax.ShapeDtypeStruct(shape, jnp.float32)


def params():
    return pltpu.CompilerParams(vmem_limit_bytes=32 * 1024 * 1024)


def solution(mesh):
    regions, blocks = mesh.devices.shape
    cores = 2
    ring = 8 if blocks % 16 == 0 else 1
    grid = Mesh(
        mesh.devices.reshape(regions, blocks // (cores * ring), ring, cores),
        ("region", "x", "y", "core"),
    )
    local = ("x", "y", "core")
    first, second = regions * cores, blocks // cores

    def shifted(value, step):
        pairs = [(i, i + step) for i in range(regions) if 0 <= i + step < regions]
        return lax.ppermute(value, "region", pairs)

    def swapped(value, pairs):
        return lax.ppermute(value, local, pairs + [(j, i) for i, j in pairs])

    def from_mate(value):
        return swapped(value, [(i, i + 1) for i in range(0, blocks - 1, 2)])

    def from_far(value):
        return swapped(value, [(i, i + 1) for i in range(1, blocks - 1, 2)])

    def on_device(pops, mask):
        hbm = pl.BlockSpec(memory_space=pltpu.HBM)
        pops, mask, to_low_y, to_high_y, to_far, to_mate = pl.pallas_call(
            pack_kernel,
            out_shape=(
                f32(19, NX, NY, 2 * LANES),
                jax.ShapeDtypeStruct((NX, NY, 2 * LANES), jnp.int32),
                f32(SLOTS, 2 * NX, 256),
                f32(SLOTS, 2 * NX, 256),
                f32(NY, 2 * LANES),
                f32(NY, 2 * LANES),
            ),
            in_specs=[hbm, hbm],
            scratch_shapes=[pltpu.SemaphoreType.DMA((NX,)), pltpu.SemaphoreType.DMA],
            compiler_params=params(),
        )(
            pltpu.with_memory_space_constraint(pops, pltpu.HBM),
            pltpu.with_memory_space_constraint(mask, pltpu.HBM),
        )
        low_y = shifted(to_high_y, 1)
        high_y = shifted(to_low_y, -1)
        far_mask = from_far(to_far)
        chip_masks = lax.all_gather(to_mate, "core")
        sums = pl.pallas_call(
            sums_kernel,
            out_shape=f32(first, 1, LANES),
            scratch_shapes=[pltpu.VMEM((2, FRONT + (NX + 2) * ROWS + 8, LANES), jnp.float32)],
            compiler_params=params(),
        )(pops, mask, low_y, high_y, far_mask, chip_masks)
        to_far, to_mate = pl.pallas_call(
            layers_kernel,
            out_shape=(f32(SLOTS, 2, 2 * ROWS, LANES), f32(SLOTS, 2, 2 * ROWS, LANES)),
            in_specs=[pl.BlockSpec(memory_space=pltpu.VMEM)] * 4 + [pl.BlockSpec(memory_space=pl.ANY)],
            compiler_params=params(),
        )(pops, mask, low_y, high_y, sums)
        far = from_far(to_far)
        mate = from_mate(to_mate)
        sums = lax.all_to_all(sums, ("region", "core"), 0, 0, tiled=True)
        sums = pl.pallas_call(
            relay_kernel,
            out_shape=f32(second, 1, LANES),
            compiler_params=params(),
            cost_estimate=pl.CostEstimate(flops=3 * 10**10, bytes_accessed=0, transcendentals=0),
        )(sums)
        sums = lax.all_to_all(sums, ("x", "y"), 0, 0, tiled=True)
        rows = FRONT + (NX + 4) * ROWS + 8
        return pl.pallas_call(
            steps_kernel,
            out_shape=pltpu.HBM((19, NX, NY, 2 * LANES), jnp.float32),
            out_specs=hbm,
            scratch_shapes=[
                pltpu.VMEM((19, 2, rows, LANES), jnp.float32),
                pltpu.VMEM((19, 2, rows, LANES), jnp.float32),
                pltpu.VMEM((2, rows, LANES), jnp.float32),
                pltpu.VMEM((NX, 19, NY, 2 * LANES), jnp.float32),
                pltpu.SemaphoreType.DMA((NX,)),
            ],
            compiler_params=params(),
        )(sums, pops, mask, low_y, high_y, far, mate)

    return jax.shard_map(
        on_device,
        mesh=grid,
        in_specs=(P(None, local, "region", None), P(local, "region", None)),
        out_specs=P(None, local, "region", None),
        check_vma=False,
    )
```
